128 devices in a mesh: group: 8 (over z, core), dev: 16 (over y, x).
Axes of the slice: x: 4, y: 4, z: 4, core: 2. Of those that a mesh axis runs over, the one named last changes fastest.
Arguments:
- positions: float32 [3, 4194304], P(None, ('group', 'dev')), may hold values from -0.5 to 2.5
- right_sides: float32 [8, 4194304], P(None, ('group', 'dev')), may hold values from -6 to 6
- leaf_basis: bfloat16 [16384, 64, 256], P(('group', 'dev')), may hold values from -0.375 to 0.375
- leaf_transfer: bfloat16 [64, 1048576], P(None, ('group', 'dev')), may hold values from -0.75 to 0.75
- far_coupling: bfloat16 [128, 128, 64, 384], P(('group', 'dev')), may hold values from -0.3125 to 0.3125
- top_transfer: float32 [254, 4096], replicated, may hold values from -0.5 to 0.5
- top_coupling: float32 [254, 4096], replicated, may hold values from -0.75 to 0.75
- near_list: int32 [16384, 6], P(('group', 'dev')), may hold values from 0 to 255, as said below
- send_leaf: int32 [128, 128, 6], P(('group', 'dev')), may hold values from 0 to 127
- send_count: int32 [128, 128], P(('group', 'dev')), may hold values from 1 to 6, as said below
- far_target: int32 [128, 128, 6], P(('group', 'dev')), may hold values from 0 to 127
Outputs:
- potential: float32 [8, 4194304], P(None, ('group', 'dev'))
The draws below stay inside these ranges and needn't reach their ends.
Inputs may be any that keep to these rules, and one draw needn't show every extreme that they name: `near_list`: every one of the 256 leaves that a device sees is named in its rows of the list. `send_count`: every sender fills all 6 slots of its message to one receiver, and every receiver gets one full message.
All inputs are finite; a program needn't handle non-finite values.
Results may differ from the reference program's by a relative error of at most 0.0042.
Values may be sent and summed in bfloat16 or wider, within the bound.
No kernel may reach another device: no remote copies, remote signals or barrier semaphores. Data moves between devices by JAX's collectives and lax.ppermute only.
A program may use at most 128 MiB of HBM per device.

```python
import math
import jax
import jax.numpy as jnp
from jax import lax

LEAF = 256
R = 64
NRHS = 8
LEAF_DEV = 128
NEAR = 6
SLOTS = 6
EDGE = 64
OWNERS = 128
NLEAVES = 16384
POINTS = 4194304
NODES = 254


def draw_positions(key, part):
    key = jax.random.fold_in(key, 5)
    center_key, jitter_key = jax.random.split(key)
    along = (jnp.arange(NLEAVES, dtype=jnp.int32).astype(jnp.float32) + 0.5) / NLEAVES
    turn = 2.0 * math.pi * 3.0 * along
    path = jnp.stack([1.0 + 0.9 * jnp.cos(turn), 1.0 + 0.9 * jnp.sin(turn), 0.1 + 1.8 * along], 0)[:, :, None]
    wobble = jax.random.uniform(center_key, (3, NLEAVES, 1), jnp.float32, -0.08, 0.08)
    jitter = jax.random.uniform(jitter_key, (3, NLEAVES, LEAF), jnp.float32, -0.32, 0.32)
    return (path + wobble + jitter).reshape(3, NLEAVES * LEAF)


def draw_near_list(key, part):
    key = jax.random.fold_in(key, 7)
    owners = NLEAVES // LEAF_DEV
    seen_leaves = LEAF_DEV + 2 * EDGE
    entries = LEAF_DEV * NEAR
    fill_key, order_key = jax.random.split(key)
    filler = jax.random.randint(fill_key, (owners, entries), 0, seen_leaves, jnp.int32)
    position = jnp.arange(entries, dtype=jnp.int32)[None, :]
    values = jnp.where(position < seen_leaves, position, filler)
    order_keys = jax.random.split(order_key, owners)
    shuffled = jax.vmap(jax.random.permutation)(order_keys, values)
    return shuffled.reshape(NLEAVES, NEAR)


def draw_send_count(key, part):
    key = jax.random.fold_in(key, 9)
    owners = NLEAVES // LEAF_DEV
    count_key, shift_key = jax.random.split(key)
    counts = jax.random.randint(count_key, (owners, owners), 1, SLOTS + 1, jnp.int32)
    offset = jax.random.randint(shift_key, (), 0, owners, jnp.int32)
    indices = jnp.arange(owners, dtype=jnp.int32)
    full_peer = (indices[:, None] + offset) % owners == indices[None, :]
    return jnp.where(full_peer, jnp.int32(SLOTS), counts)


def place_ends(values, own_key, least, high):
    shape = values.shape
    spot = [jax.random.randint(jax.random.fold_in(own_key, axis), (), 0, shape[axis]) for axis in range(len(shape))]
    values = values.at[tuple(spot)].set(least)
    longest = shape.index(max(shape))
    spot[longest] = (spot[longest] + 1) % shape[longest]
    return values.at[tuple(spot)].set(high)


def block_scale(own_key, dims, pieces, smallest, top_value):
    def one(dim, shards_of):
        steps = jax.random.uniform(jax.random.fold_in(jax.random.fold_in(own_key, 6), dim), (shards_of,), jnp.float32, smallest / len(pieces), top_value / len(pieces))
        return jnp.repeat(jnp.exp(steps), dims[dim] // shards_of).reshape((-1,) + (1,) * (len(dims) - dim - 1))

    level = one(*pieces[0])
    for cut in pieces[1:]:
        level = level * one(*cut)
    return level


def noise(stream_key, dims, width, reach, pieces=(), kind=jnp.bfloat16):
    array = jax.random.normal(stream_key, dims, jnp.float32) * width
    if len(pieces) > 0:
        array = block_scale(stream_key, dims, pieces, -0.22, 0.18) * array
    return jnp.clip(array, min=-reach, max=reach).astype(kind)


def setup_inputs(seed: int = 0) -> dict:
    keys = jax.random.split(jax.random.key(seed), 12)
    positions = draw_positions(jax.random.fold_in(keys[11], 71), 0)
    right_sides = noise(keys[1], (NRHS, POINTS), 1.0, 6.0, ((1, 128),), jnp.float32)
    leaf_basis = noise(keys[2], (NLEAVES, R, LEAF), LEAF ** -0.5, 0.375, ((0, 128),))
    leaf_transfer = noise(keys[3], (R, NLEAVES * R), R ** -0.5, 0.75, ((1, 128),))
    far_coupling = noise(keys[4], (OWNERS, OWNERS, R, SLOTS * R), (R * SLOTS) ** -0.5, 0.3125, ((0, 128),))
    top_transfer = noise(keys[5], (NODES, R * R), (2 * R) ** -0.5, 0.5, (), jnp.float32)
    top_coupling = noise(keys[6], (NODES, R * R), R ** -0.5, 0.75, (), jnp.float32)
    near_list = draw_near_list(jax.random.fold_in(keys[11], 71), 0)
    send_leaf = place_ends(jax.random.randint(keys[8], (OWNERS, OWNERS, SLOTS), 0, LEAF_DEV), jax.random.fold_in(keys[8], 1), 0, LEAF_DEV - 1).astype(jnp.int32)
    send_count = draw_send_count(jax.random.fold_in(keys[11], 71), 0)
    far_target = place_ends(jax.random.randint(keys[10], (OWNERS, OWNERS, SLOTS), 0, LEAF_DEV), jax.random.fold_in(keys[10], 1), 0, LEAF_DEV - 1).astype(jnp.int32)
    return dict(positions=positions, right_sides=right_sides, leaf_basis=leaf_basis, leaf_transfer=leaf_transfer, far_coupling=far_coupling, top_transfer=top_transfer, top_coupling=top_coupling, near_list=near_list, send_leaf=send_leaf, send_count=send_count, far_target=far_target)


kernel_scale = 0.25 / (4.0 * math.pi)
smoothing = 0.0025

def near_field(own_points, seen_points, seen_values, near_rows):
    leaves = near_rows.shape[0]
    group_size = math.gcd(leaves, 8)
    leaf_width = own_points.shape[2]

    def one_group(first_leaf):
        picked = lax.dynamic_slice_in_dim(near_rows, first_leaf, group_size, 0)
        target_points = lax.dynamic_slice_in_dim(own_points, first_leaf, group_size, 1)
        source_points = seen_points[:, picked]
        source_values = seen_values[:, picked]
        distance = jnp.zeros(picked.shape + (leaf_width, leaf_width), jnp.float32)
        for component in range(3):
            difference = target_points[component][:, None, :, None] - source_points[component][:, :, None, :]
            distance = distance + difference * difference
        kernel = (kernel_scale / jnp.sqrt(distance + smoothing)).astype(jnp.bfloat16)
        kernel = lax.optimization_barrier(kernel)
        return jnp.einsum('gkpq,ngkq->ngp', kernel.astype(jnp.float32), source_values.astype(jnp.float32))
    starts = jnp.arange(leaves // group_size, dtype=jnp.int32) * group_size
    blocks = lax.map(one_group, starts)
    return blocks.transpose(1, 0, 2, 3).reshape(seen_values.shape[0], leaves, leaf_width)

def reference(positions, right_sides, leaf_basis, leaf_transfer, far_coupling, top_transfer, top_coupling, near_list, send_leaf, send_count, far_target):
    highest = lax.Precision.HIGHEST
    owners = NLEAVES // LEAF_DEV
    levels = owners.bit_length() - 1
    rounded = right_sides.astype(jnp.bfloat16)
    rounded = lax.optimization_barrier(rounded)
    moments = jnp.einsum('lrp,nlp->lnr', leaf_basis.astype(jnp.float32), rounded.reshape(NRHS, NLEAVES, LEAF).astype(jnp.float32)).astype(jnp.bfloat16)
    moments = lax.optimization_barrier(moments)
    transfer_leaf = leaf_transfer.reshape(R, owners, LEAF_DEV, R).astype(jnp.float32)
    device_moment = jnp.einsum('dlnb,bdla->dna', moments.reshape(owners, LEAF_DEV, NRHS, R).astype(jnp.float32), transfer_leaf)
    device_moment = device_moment * (1.0 / math.sqrt(LEAF_DEV))
    transfer_table = top_transfer.reshape(NODES, R, R)
    coupling_table = top_coupling.reshape(NODES, R, R)
    level_moments = [device_moment]
    for level_index in range(levels):
        cluster_count = owners >> level_index
        node_base = 2 * owners - 2 * cluster_count
        halves = jnp.einsum('cnb,cba->cna', level_moments[level_index], transfer_table[node_base:node_base + cluster_count], precision=highest)
        level_moments.append(halves[0::2] + halves[1::2])
    local_field = jnp.zeros((1, NRHS, R), jnp.float32)
    for level_index in reversed(range(levels)):
        cluster_count = owners >> level_index
        node_base = 2 * owners - 2 * cluster_count
        current = level_moments[level_index]
        sibling = current.reshape(cluster_count // 2, 2, NRHS, R)[:, ::-1].reshape(cluster_count, NRHS, R)
        coupling_term = jnp.einsum('cnb,cab->cna', sibling, coupling_table[node_base:node_base + cluster_count], precision=highest)
        parent_field = jnp.repeat(local_field, 2, axis=0)
        local_field = coupling_term + jnp.einsum('cnb,cab->cna', parent_field, transfer_table[node_base:node_base + cluster_count], precision=highest)
    device_field = local_field.astype(jnp.bfloat16)
    device_field = lax.optimization_barrier(device_field)
    device_local = jnp.einsum('bdla,dna->dlnb', transfer_leaf, device_field.astype(jnp.float32))
    flat_moments = moments.reshape(NLEAVES, NRHS * R)
    source_leaf = jnp.arange(owners, dtype=jnp.int32)[:, None, None] * LEAF_DEV + send_leaf
    live_slots = jnp.arange(SLOTS, dtype=jnp.int32)[None, None, :] < send_count[:, :, None]
    sent = jnp.where(live_slots[..., None], flat_moments[source_leaf], jnp.zeros((), jnp.bfloat16))
    received = sent.transpose(1, 0, 2, 3)

    def far_one(items):
        coupling_rows, target_rows, arrived = items
        coupling_blocks = coupling_rows.reshape(owners, R, SLOTS, R).astype(jnp.float32)
        arrived_blocks = arrived.reshape(owners, SLOTS, NRHS, R).astype(jnp.float32)
        contrib = jnp.einsum('pasb,psnb->psna', coupling_blocks, arrived_blocks)
        targets = (target_rows[:, :, None] == jnp.arange(LEAF_DEV, dtype=jnp.int32)[None, None, :]).astype(jnp.float32)
        return jnp.einsum('psl,psna->lna', targets, contrib, precision=highest)
    far_local = lax.map(far_one, (far_coupling, far_target, received))
    leaf_local = (device_local + far_local).astype(jnp.bfloat16).reshape(NLEAVES, NRHS, R)
    leaf_local = lax.optimization_barrier(leaf_local)
    far_potential = jnp.einsum('lbp,lnb->nlp', leaf_basis.astype(jnp.float32), leaf_local.astype(jnp.float32))
    rim_width = EDGE * LEAF
    padded_points = jnp.pad(positions, ((0, 0), (rim_width, rim_width)))
    padded_values = jnp.pad(rounded, ((0, 0), (rim_width, rim_width)))
    seen_leaves = LEAF_DEV + 2 * EDGE
    self_rows = (jnp.arange(LEAF_DEV, dtype=jnp.int32) + EDGE)[:, None]

    def near_one(owner_index):
        first_point = owner_index * (LEAF_DEV * LEAF)
        seen_points = lax.dynamic_slice_in_dim(padded_points, first_point, seen_leaves * LEAF, 1).reshape(3, seen_leaves, LEAF)
        seen_values = lax.dynamic_slice_in_dim(padded_values, first_point, seen_leaves * LEAF, 1).reshape(NRHS, seen_leaves, LEAF)
        own_points = seen_points[:, EDGE:EDGE + LEAF_DEV]
        listed = lax.dynamic_slice_in_dim(near_list, owner_index * LEAF_DEV, LEAF_DEV, 0)
        near_rows = jnp.concatenate([self_rows, listed], 1)
        return near_field(own_points, seen_points, seen_values, near_rows)
    near_parts = lax.map(near_one, jnp.arange(owners, dtype=jnp.int32))
    near_potential = near_parts.transpose(1, 0, 2, 3).reshape(NRHS, NLEAVES, LEAF)
    potential = far_potential + near_potential
    return potential.reshape(NRHS, POINTS)
```

```python
import functools
import math

import jax
import jax.numpy as jnp
from jax import lax
from jax.experimental import pallas as pl
from jax.experimental.pallas import tpu as pltpu
from jax.sharding import PartitionSpec as P

LEAF = 256
R = 64
N = 8
EDGE = 64
OWN = 128
SEEN = 256
SLOTS = 6
NEAR = 6
FEAT = 48
F32 = jnp.float32
BF16 = jnp.bfloat16

kernel_scale = 0.25 / (4.0 * math.pi)
smoothing = 0.0025
inverse_scale = 1.0 / kernel_scale

NN = (((1,), (0,)), ((), ()))
NT = (((1,), (1,)), ((), ()))
VMEM = pl.BlockSpec(memory_space=pltpu.VMEM)
SMEM = pl.BlockSpec(memory_space=pltpu.SMEM)
ANY = pl.BlockSpec(memory_space=pl.ANY)


def dot(a, b, dims=NN):
    return lax.dot_general(a, b, dims, preferred_element_type=F32)


def exact_dot(a, b, dims=NN):
    return lax.dot_general(a, b, dims, precision=lax.Precision.HIGHEST, preferred_element_type=F32)


def aligned(index, size):
    return pl.ds(pl.multiple_of(index * size, size), size)


def params(megabytes):
    return pltpu.CompilerParams(vmem_limit_bytes=megabytes << 20)


def round16(x):
    return x.astype(BF16).astype(F32)


def features(points, is_target):
    width = points.shape[1]
    row = lax.broadcasted_iota(jnp.int32, (8, width), 0)
    padded = jnp.concatenate([points, jnp.ones((5, width), F32)], 0)
    x = jnp.where(row < 3, (padded - 1.0) * inverse_scale, 0.0)
    high = round16(x)
    low = round16(x - high)
    x = high + low
    square = jnp.broadcast_to(jnp.sum(x * x, axis=0, keepdims=True), (8, width))
    if is_target:
        square = square + smoothing * inverse_scale * inverse_scale
    s0 = round16(square)
    s1 = round16(square - s0)
    s2 = square - s0 - s1
    zero = jnp.zeros_like(x)
    if is_target:
        last = jnp.where(row == 0, s0, jnp.where(row == 1, s1, jnp.where(row == 2, s2, jnp.where(row < 6, 1.0, 0.0))))
        parts = [-2.0 * high, -2.0 * high, -2.0 * low, -2.0 * low, last, zero]
    else:
        last = jnp.where(row < 3, 1.0, jnp.where(row == 3, s0, jnp.where(row == 4, s1, jnp.where(row == 5, s2, 0.0))))
        parts = [high, low, high, low, last, zero]
    return jnp.concatenate(parts, 0)


def inverse_root(distance):
    return lax.rsqrt(distance.astype(BF16))


def moment_kernel(send_leaf, send_count, values, basis, transfer, message, device_moment, moments):
    def four_leaves(g, total):
        picked = []
        for j in range(4):
            leaf = g * 4 + j
            v = values[:, aligned(leaf, LEAF)].astype(BF16)
            m = round16(dot(v, basis[leaf], NT))
            moments[leaf] = jnp.concatenate([m, m], 1)
            picked.append(m)
        return total + dot(jnp.concatenate(picked, 0).astype(BF16), transfer[:, aligned(g, 4 * R)])

    total = lax.fori_loop(0, OWN // 4, four_leaves, jnp.zeros((4 * N, 4 * R), F32))
    moment = total[0:N, 0:R]
    for j in range(1, 4):
        moment = moment + total[j * N : (j + 1) * N, j * R : (j + 1) * R]
    device_moment[...] = moment * (1.0 / math.sqrt(OWN))

    is_left = lax.broadcasted_iota(jnp.int32, (N, 2 * R), 1) < R

    def two_receivers(g, carry):
        rows = []
        for j in range(2):
            p = g * 2 + j
            count = send_count[0, p]
            for pair in range(SLOTS // 2):
                left = moments[send_leaf[2 * pair, p]]
                right = moments[send_leaf[2 * pair + 1, p]]
                left = jnp.where(2 * pair < count, left, 0.0)
                right = jnp.where(2 * pair + 1 < count, right, 0.0)
                rows.append(jnp.where(is_left, left, right))
        message[aligned(g, 48), :] = jnp.concatenate(rows, 0).astype(BF16)
        return carry

    lax.fori_loop(0, OWN // 2, two_receivers, 0, unroll=2)


def self_kernel(points, values, out):
    def four_leaves(g, carry):
        kernels = []
        for j in range(4):
            x = points[:, aligned(g * 4 + j, LEAF)]
            target = features(x, True).astype(BF16)
            source = features(x, False).T.astype(BF16)
            kernels.append(inverse_root(dot(source, target)))
        for j in range(4):
            v = values[:, aligned(g * 4 + j, LEAF)].astype(BF16)
            out[:, aligned(g * 4 + j, LEAF)] = dot(v, kernels[j])
        return carry

    lax.fori_loop(0, OWN // 4, four_leaves, 0)


def near_kernel(
    near_list, points_below, points, points_above, values_below, values, values_above, before, out,
    sources, targets, seen_values,
):
    def stage(point_ref, value_ref, first, count, own):
        def one(i, carry):
            x = point_ref[:, aligned(i, LEAF)]
            sources[first + i] = features(x, False).T.astype(BF16)
            seen_values[first + i] = value_ref[:, aligned(i, LEAF)]
            if own:
                targets[i] = features(x, True).astype(BF16)
            return carry

        lax.fori_loop(0, count, one, 0, unroll=2)

    stage(points_below, values_below, 0, EDGE, False)
    stage(points, values, EDGE, OWN, True)
    stage(points_above, values_above, EDGE + OWN, EDGE, False)

    def two_leaves(g, carry):
        for j in range(2):
            leaf = g * 2 + j
            target = targets[leaf]
            seen = [near_list[k, leaf] for k in range(NEAR)]
            kernels = [inverse_root(dot(sources[e], target)) for e in seen]
            total = before[:, aligned(leaf, LEAF)]
            for k in range(NEAR):
                total = total + dot(seen_values[seen[k]].astype(BF16), kernels[k])
            out[:, aligned(leaf, LEAF)] = total
        return carry

    lax.fori_loop(0, OWN // 2, two_leaves, 0)


def fetch(table, row, matrices, slot):
    flat = table[pl.ds(row, 1), :]
    for j in range(R // 2):
        pair = flat[:, j * 2 * R : (j + 1) * 2 * R]
        matrices[slot, 2 * j : 2 * j + 1, 0:R] = pair[:, 0:R]
        matrices[slot, 2 * j + 1 : 2 * j + 2, 0:R] = pair[:, R : 2 * R]


def upward(ups, matrices, slot):
    result = []
    for c in range(0, len(ups), 2):
        left = exact_dot(ups[c], matrices[slot + c])
        result.append(left + exact_dot(ups[c + 1], matrices[slot + c + 1]))
    return result


def group_tree_kernel(place, gathered, table, siblings, group_moment, matrices, levels_ref):
    group = place[0]
    dev = place[1]
    slot = 0
    ups = [gathered[c * N : (c + 1) * N, :] for c in range(16)]
    first = [0]
    for level in range(4):
        count = 16 >> level
        base = 2 * OWN - 2 * (OWN >> level)

        def fill(i, carry):
            fetch(table, base + group * count + i, matrices, slot + i)
            return carry

        lax.fori_loop(0, count, fill, 0)
        slot += count
    slot = 0
    for level in range(4):
        count = 16 >> level
        for c in range(count):
            levels_ref[slot + c] = ups[c]
        siblings[level] = levels_ref[slot + ((dev >> level) ^ 1)]
        ups = upward(ups, matrices, slot)
        slot += count
    group_moment[...] = ups[0]


def far_kernel(
    place, far_target, incoming, siblings, group_moments, near,
    coupling_hbm, transfer_hbm, basis_hbm, top_transfer_hbm, top_coupling_hbm,
    out,
    coupling, transfer, basis, top_transfer, top_coupling, far_local, matrices, levels_ref, sems,
):
    chunks = 4
    chunk = OWN // chunks
    copies = []
    for i in range(chunks):
        copies.append(pltpu.make_async_copy(coupling_hbm.at[pl.ds(i * chunk, chunk)], coupling.at[pl.ds(i * chunk, chunk)], sems.at[i]))
    rest = [(top_transfer_hbm, top_transfer), (top_coupling_hbm, top_coupling), (transfer_hbm, transfer), (basis_hbm, basis)]
    for i, (source, target) in enumerate(rest):
        copies.append(pltpu.make_async_copy(source, target, sems.at[chunks + i]))
    for copy in copies:
        copy.start()

    far_local[...] = jnp.zeros_like(far_local)
    is_left = lax.broadcasted_iota(jnp.int32, (N, 2 * R), 1) < R

    for i in range(chunks):
        copies[i].wait()

        def two_senders(g, carry):
            arrived = incoming[aligned(g, 48), :].astype(F32)
            results = []
            for j in range(2):
                p = g * 2 + j
                for pair in range(SLOTS // 2):
                    tile = arrived[(j * 3 + pair) * N : (j * 3 + pair + 1) * N, :]
                    left = jnp.where(is_left, tile, 0.0)
                    right = jnp.where(is_left, 0.0, tile)
                    both = jnp.concatenate([left, right], 0).astype(BF16)
                    matrix = coupling[p, :, pair * 2 * R : (pair + 1) * 2 * R]
                    results.append(dot(both, matrix, NT))
            for j in range(2):
                p = g * 2 + j
                for slot in range(SLOTS):
                    leaf = far_target[slot, p]
                    part = results[j * 3 + slot // 2][(slot % 2) * N : (slot % 2 + 1) * N, :]
                    far_local[leaf] = far_local[leaf] + part
            return carry

        lax.fori_loop(i * chunk // 2, (i + 1) * chunk // 2, two_senders, 0, unroll=2)

    group = place[0]
    owner = group * 16 + place[1]
    copies[chunks].wait()
    copies[chunks + 1].wait()

    def fill_top(i, carry):
        fetch(top_transfer, 240 + i, matrices, i)
        return carry

    lax.fori_loop(0, 12, fill_top, 0)
    for level in range(7):
        node = 2 * OWN - 2 * (OWN >> level) + (owner >> level)
        fetch(top_coupling, node, matrices, 12 + level)
        if level < 6:
            fetch(top_transfer, node, matrices, 19 + level)
    sibling_moments = [siblings[level] for level in range(4)]
    ups = [group_moments[c * N : (c + 1) * N, :] for c in range(8)]
    slot = 0
    for level in range(3):
        count = 8 >> level
        for c in range(count):
            levels_ref[slot + c] = ups[c]
        sibling_moments.append(levels_ref[slot + ((group >> level) ^ 1)])
        if level < 2:
            ups = upward(ups, matrices, slot)
        slot += count
    field = exact_dot(sibling_moments[6], matrices[12 + 6], NT)
    for level in reversed(range(6)):
        coupled = exact_dot(sibling_moments[level], matrices[12 + level], NT)
        field = coupled + exact_dot(field, matrices[19 + level], NT)
    field = round16(field)

    wide = jnp.concatenate([jnp.concatenate([field] * 4, 1)] * 4, 0)
    row_leaf = lax.broadcasted_iota(jnp.int32, (4 * N, 4 * R), 0) // N
    column_leaf = lax.broadcasted_iota(jnp.int32, (4 * N, 4 * R), 1) // R
    fields = jnp.where(row_leaf == column_leaf, wide, 0.0).astype(BF16)
    copies[chunks + 2].wait()
    copies[chunks + 3].wait()

    def four_leaves(g, carry):
        local = dot(fields, transfer[:, aligned(g, 4 * R)], NT)
        for j in range(4):
            leaf = g * 4 + j
            total = (local[j * N : (j + 1) * N, :] + far_local[leaf]).astype(BF16)
            out[:, aligned(leaf, LEAF)] = near[:, aligned(leaf, LEAF)] + dot(total, basis[leaf])
        return carry

    lax.fori_loop(0, OWN // 4, four_leaves, 0, unroll=2)


def from_behind(block, axis, distance):
    devices = range(lax.axis_size(axis))
    route = [(i - distance, i) for i in devices if i - distance in devices]
    return lax.ppermute(block, axis, route)


def shards(
    positions, right_sides, leaf_basis, leaf_transfer, far_coupling, top_transfer, top_coupling,
    near_list, send_leaf, send_count, far_target,
):
    both = ("group", "dev")
    points = OWN * LEAF
    rim = EDGE * LEAF
    place = jnp.stack([lax.axis_index("group"), lax.axis_index("dev")]).astype(jnp.int32)
    rounded = right_sides.astype(BF16)
    values_below = from_behind(rounded[:, points - rim :], both, 1)
    values_above = from_behind(rounded[:, :rim], both, -1)
    points_below = from_behind(positions[:, points - rim :], both, 1)
    points_above = from_behind(positions[:, :rim], both, -1)

    message, device_moment = pl.pallas_call(
        moment_kernel,
        out_shape=(jax.ShapeDtypeStruct((OWN * 24, 2 * R), BF16), jax.ShapeDtypeStruct((N, R), F32)),
        in_specs=[SMEM, SMEM, VMEM, VMEM, VMEM],
        out_specs=(VMEM, VMEM),
        scratch_shapes=[pltpu.VMEM((OWN, N, 2 * R), F32)],
        compiler_params=params(32),
        cost_estimate=pl.CostEstimate(flops=10**9, bytes_accessed=8 << 20, transcendentals=0),
        name="moments",
    )(send_leaf[0].T, send_count, right_sides, leaf_basis, leaf_transfer)

    gathered = lax.all_gather(device_moment, "dev", axis=0, tiled=True)
    incoming = lax.all_to_all(message, both, split_axis=0, concat_axis=0, tiled=True)

    near_self = pl.pallas_call(
        self_kernel,
        out_shape=jax.ShapeDtypeStruct((N, points), F32),
        in_specs=[VMEM, VMEM],
        out_specs=VMEM,
        compiler_params=params(32),
        cost_estimate=pl.CostEstimate(flops=8 * 10**9, bytes_accessed=3 << 20, transcendentals=0),
        name="near_self",
    )(positions, right_sides)

    gathered, near_self = lax.optimization_barrier((gathered, near_self))
    siblings, group_moment = pl.pallas_call(
        group_tree_kernel,
        out_shape=(jax.ShapeDtypeStruct((4, N, R), F32), jax.ShapeDtypeStruct((N, R), F32)),
        in_specs=[SMEM, VMEM, VMEM],
        out_specs=(VMEM, VMEM),
        scratch_shapes=[pltpu.VMEM((30, R, R), F32), pltpu.VMEM((30, N, R), F32)],
        compiler_params=params(32),
        cost_estimate=pl.CostEstimate(flops=10**8, bytes_accessed=4 << 20, transcendentals=0),
        name="group_tree",
    )(place, gathered, top_transfer)
    group_moments = lax.all_gather(group_moment, "group", axis=0, tiled=True)
    near_self, siblings = lax.optimization_barrier((near_self, siblings))

    near = pl.pallas_call(
        near_kernel,
        out_shape=jax.ShapeDtypeStruct((N, points), F32),
        in_specs=[SMEM] + [VMEM] * 7,
        out_specs=VMEM,
        scratch_shapes=[
            pltpu.VMEM((SEEN, LEAF, FEAT), BF16),
            pltpu.VMEM((OWN, FEAT, LEAF), BF16),
            pltpu.VMEM((SEEN, N, LEAF), F32),
        ],
        compiler_params=params(56),
        cost_estimate=pl.CostEstimate(flops=60 * 10**9, bytes_accessed=6 << 20, transcendentals=0),
        name="near_listed",
    )(
        near_list.T, points_below, positions, points_above,
        values_below.astype(F32), right_sides, values_above.astype(F32), near_self,
    )

    return pl.pallas_call(
        far_kernel,
        out_shape=jax.ShapeDtypeStruct((N, points), F32),
        in_specs=[SMEM, SMEM, VMEM, VMEM, VMEM, VMEM, ANY, ANY, ANY, ANY, ANY],
        out_specs=VMEM,
        scratch_shapes=[
            pltpu.VMEM((OWN, R, SLOTS * R), BF16),
            pltpu.VMEM((R, OWN * R), BF16),
            pltpu.VMEM((OWN, R, LEAF), BF16),
            pltpu.VMEM((254, R * R), F32),
            pltpu.VMEM((254, R * R), F32),
            pltpu.VMEM((OWN, N, R), F32),
            pltpu.VMEM((25, R, R), F32),
            pltpu.VMEM((14, N, R), F32),
            pltpu.SemaphoreType.DMA((8,)),
        ],
        compiler_params=params(56),
        cost_estimate=pl.CostEstimate(flops=2 * 10**9, bytes_accessed=22 << 20, transcendentals=0),
        name="far_field",
    )(
        place, far_target[0].T, incoming, siblings, group_moments, near,
        far_coupling[0], leaf_transfer, leaf_basis, top_transfer, top_coupling,
    )


def solution(mesh):
    both = ("group", "dev")
    placed = (
        P(None, both), P(None, both), P(both, None, None), P(None, both), P(both, None, None, None),
        P(), P(), P(both, None), P(both, None, None), P(both, None), P(both, None, None),
    )
    return jax.shard_map(shards, mesh=mesh, in_specs=placed, out_specs=P(None, both), check_vma=False)
```

```python
import functools
import math

import jax
import jax.numpy as jnp
from jax import lax
from jax.experimental import pallas as pl
from jax.experimental.pallas import tpu as pltpu
from jax.sharding import PartitionSpec as P

LEAF = 256
R = 64
N = 8
EDGE = 64
OWN = 128
SEEN = 256
SLOTS = 6
NEAR = 6
FEAT = 48
F32 = jnp.float32
BF16 = jnp.bfloat16

kernel_scale = 0.25 / (4.0 * math.pi)
smoothing = 0.0025
inverse_scale = 1.0 / kernel_scale

NN = (((1,), (0,)), ((), ()))
NT = (((1,), (1,)), ((), ()))
VMEM = pl.BlockSpec(memory_space=pltpu.VMEM)
SMEM = pl.BlockSpec(memory_space=pltpu.SMEM)
ANY = pl.BlockSpec(memory_space=pl.ANY)


def dot(a, b, dims=NN):
    return lax.dot_general(a, b, dims, preferred_element_type=F32)


def exact_dot(a, b, dims=NN):
    return lax.dot_general(a, b, dims, precision=lax.Precision.HIGHEST, preferred_element_type=F32)


def aligned(index, size):
    return pl.ds(pl.multiple_of(index * size, size), size)


def params(megabytes):
    return pltpu.CompilerParams(vmem_limit_bytes=megabytes << 20)


def round16(x):
    return x.astype(BF16).astype(F32)


def split_points(points):
    width = points.shape[1]
    row = lax.broadcasted_iota(jnp.int32, (8, width), 0)
    padded = jnp.concatenate([points, jnp.ones((5, width), F32)], 0)
    x = jnp.where(row < 3, (padded - 1.0) * inverse_scale, 0.0)
    high = round16(x)
    return high, round16(x - high)


def features(high, low, is_target):
    width = high.shape[1]
    row = lax.broadcasted_iota(jnp.int32, (8, width), 0)
    x = high + low
    square = jnp.broadcast_to(jnp.sum(x * x, axis=0, keepdims=True), (8, width))
    if is_target:
        square = square + smoothing * inverse_scale * inverse_scale
    s0 = round16(square)
    s1 = round16(square - s0)
    s2 = square - s0 - s1
    zero = jnp.zeros_like(x)
    if is_target:
        last = jnp.where(row == 0, s0, jnp.where(row == 1, s1, jnp.where(row == 2, s2, jnp.where(row < 6, 1.0, 0.0))))
        parts = [-2.0 * high, -2.0 * high, -2.0 * low, -2.0 * low, last, zero]
    else:
        last = jnp.where(row < 3, 1.0, jnp.where(row == 3, s0, jnp.where(row == 4, s1, jnp.where(row == 5, s2, 0.0))))
        parts = [high, low, high, low, last, zero]
    return jnp.concatenate(parts, 0)


def inverse_root(distance):
    return lax.rsqrt(distance.astype(BF16))


def pack_kernel(points, values, first, last):
    rim = EDGE * LEAF
    for out, start in ((first, 0), (last, OWN * LEAF - rim)):

        def one(i, carry):
            columns = pl.ds(pl.multiple_of(start + i * 4 * LEAF, LEAF), 4 * LEAF)
            high, low = split_points(points[:, columns])
            both = high + pltpu.roll(low, 3, 0)
            out[:, aligned(i, 4 * LEAF)] = jnp.concatenate([values[:, columns], both], 0).astype(BF16)
            return carry

        lax.fori_loop(0, EDGE // 4, one, 0)


def moment_kernel(
    place, send_leaf, send_count, values, basis_hbm, transfer, top_transfer_hbm,
    message, basis, top_transfer, moments, chain, matrices, sems,
):
    chunks = 4
    chunk = OWN // chunks
    copies = []
    for i in range(chunks):
        copies.append(pltpu.make_async_copy(basis_hbm.at[pl.ds(i * chunk, chunk)], basis.at[pl.ds(i * chunk, chunk)], sems.at[i]))
    copies.append(pltpu.make_async_copy(top_transfer_hbm, top_transfer, sems.at[chunks]))
    for copy in copies:
        copy.start()
    owner = place[0]

    def four_leaves(g, total):
        picked = []
        for j in range(4):
            leaf = g * 4 + j
            v = values[:, aligned(leaf, LEAF)].astype(BF16)
            m = round16(dot(v, basis[leaf], NT))
            moments[leaf] = jnp.concatenate([m, m], 1)
            picked.append(m)
        return total + dot(jnp.concatenate(picked, 0).astype(BF16), transfer[:, aligned(g, 4 * R)])

    total = jnp.zeros((4 * N, 4 * R), F32)
    for i in range(chunks):
        copies[i].wait()
        total = lax.fori_loop(i * chunk // 4, (i + 1) * chunk // 4, four_leaves, total, unroll=2)
    current = total[0:N, 0:R]
    for j in range(1, 4):
        current = current + total[j * N : (j + 1) * N, j * R : (j + 1) * R]
    current = current * (1.0 / math.sqrt(OWN))

    copies[chunks].wait()
    for level in range(6):
        fetch(top_transfer, 2 * OWN - 2 * (OWN >> level) + (owner >> level), matrices, level)
    for level in range(7):
        high = round16(current)
        chain[level] = jnp.concatenate([high, current - high], 1)
        if level < 6:
            current = exact_dot(current, matrices[level])

    is_left = lax.broadcasted_iota(jnp.int32, (N, 2 * R), 1) < R

    def one_receiver(p, carry):
        rows = []
        count = send_count[0, p]
        for pair in range(SLOTS // 2):
            left = moments[send_leaf[2 * pair, p]]
            right = moments[send_leaf[2 * pair + 1, p]]
            left = jnp.where(2 * pair < count, left, 0.0)
            right = jnp.where(2 * pair + 1 < count, right, 0.0)
            rows.append(jnp.where(is_left, left, right))
        rows.append(chain[top_bit(owner ^ p)])
        message[aligned(p, 4 * N), :] = jnp.concatenate(rows, 0).astype(BF16)
        return carry

    lax.fori_loop(0, OWN, one_receiver, 0, unroll=4)


def top_bit(x):
    return sum((x >= (1 << j)).astype(jnp.int32) for j in range(1, 7))


def near_kernel(
    near_list, below, points, values, above, out, sources, targets, seen_values,
):
    def rim(ref, first):
        row = lax.broadcasted_iota(jnp.int32, (N, LEAF), 0)

        def one(i, carry):
            block = ref[:, aligned(i, LEAF)].astype(F32)
            both = block[N:, :]
            high = jnp.where(row < 3, both, 0.0)
            low = jnp.where(row < 3, pltpu.roll(both, 5, 0), 0.0)
            sources[first + i] = features(high, low, False).T.astype(BF16)
            seen_values[first + i] = block[:N, :]
            return carry

        lax.fori_loop(0, EDGE, one, 0, unroll=2)

    def own(i, carry):
        high, low = split_points(points[:, aligned(i, LEAF)])
        sources[EDGE + i] = features(high, low, False).T.astype(BF16)
        targets[i] = features(high, low, True).astype(BF16)
        seen_values[EDGE + i] = values[:, aligned(i, LEAF)]
        return carry

    lax.fori_loop(0, OWN, own, 0, unroll=2)
    rim(below, 0)
    rim(above, EDGE + OWN)

    def two_leaves(g, carry):
        for j in range(2):
            leaf = g * 2 + j
            target = targets[leaf]
            seen = [EDGE + leaf] + [near_list[k, leaf] for k in range(NEAR)]
            kernels = [inverse_root(dot(sources[e], target)) for e in seen]
            total = jnp.zeros((N, LEAF), F32)
            for e, kernel in zip(seen, kernels):
                total = total + dot(seen_values[e].astype(BF16), kernel)
            out[:, aligned(leaf, LEAF)] = total
        return carry

    lax.fori_loop(0, OWN // 2, two_leaves, 0)


def fetch(table, row, matrices, slot):
    flat = table[pl.ds(row, 1), :]
    for j in range(R // 2):
        pair = flat[:, j * 2 * R : (j + 1) * 2 * R]
        matrices[slot, 2 * j : 2 * j + 1, 0:R] = pair[:, 0:R]
        matrices[slot, 2 * j + 1 : 2 * j + 2, 0:R] = pair[:, R : 2 * R]


def far_kernel(
    place, far_target, incoming, near,
    coupling_hbm, transfer_hbm, basis_hbm, top_transfer_hbm, top_coupling_hbm,
    out,
    coupling, transfer, basis, top_transfer, top_coupling, far_local, matrices, siblings, sems,
):
    chunks = 4
    chunk = OWN // chunks
    copies = []
    for i in range(chunks):
        copies.append(pltpu.make_async_copy(coupling_hbm.at[pl.ds(i * chunk, chunk)], coupling.at[pl.ds(i * chunk, chunk)], sems.at[i]))
    rest = [(top_transfer_hbm, top_transfer), (top_coupling_hbm, top_coupling), (transfer_hbm, transfer), (basis_hbm, basis)]
    for i, (source, target) in enumerate(rest):
        copies.append(pltpu.make_async_copy(source, target, sems.at[chunks + i]))
    for copy in copies:
        copy.start()

    owner = place[0]
    far_local[...] = jnp.zeros_like(far_local)
    siblings[...] = jnp.zeros_like(siblings)
    is_left = lax.broadcasted_iota(jnp.int32, (N, 2 * R), 1) < R

    for i in range(chunks):
        copies[i].wait()

        def two_senders(g, carry):
            arrived = incoming[aligned(g, 64), :].astype(F32)
            results = []
            for j in range(2):
                p = g * 2 + j
                for pair in range(SLOTS // 2):
                    tile = arrived[(j * 4 + pair) * N : (j * 4 + pair + 1) * N, :]
                    left = jnp.where(is_left, tile, 0.0)
                    right = jnp.where(is_left, 0.0, tile)
                    both = jnp.concatenate([left, right], 0).astype(BF16)
                    matrix = coupling[p, :, pair * 2 * R : (pair + 1) * 2 * R]
                    results.append(dot(both, matrix, NT))
            for j in range(2):
                p = g * 2 + j
                level = jnp.where(p == owner, 7, top_bit(owner ^ p))
                siblings[level] = siblings[level] + arrived[(j * 4 + 3) * N : (j * 4 + 4) * N, :]
                for slot in range(SLOTS):
                    leaf = far_target[slot, p]
                    part = results[j * 3 + slot // 2][(slot % 2) * N : (slot % 2 + 1) * N, :]
                    far_local[leaf] = far_local[leaf] + part
            return carry

        lax.fori_loop(i * chunk // 2, (i + 1) * chunk // 2, two_senders, 0, unroll=2)

    copies[chunks].wait()
    copies[chunks + 1].wait()
    for level in range(7):
        node = 2 * OWN - 2 * (OWN >> level) + (owner >> level)
        fetch(top_coupling, node, matrices, level)
        if level < 6:
            fetch(top_transfer, node, matrices, 7 + level)
    coupled = []
    for level in range(7):
        both = siblings[level]
        coupled.append(exact_dot(both[:, :R] + both[:, R:], matrices[level], NT))
    field = coupled[6]
    for level in reversed(range(6)):
        field = coupled[level] + exact_dot(field, matrices[7 + level], NT)
    field = round16(field)

    wide = jnp.concatenate([jnp.concatenate([field] * 4, 1)] * 4, 0)
    row_leaf = lax.broadcasted_iota(jnp.int32, (4 * N, 4 * R), 0) // N
    column_leaf = lax.broadcasted_iota(jnp.int32, (4 * N, 4 * R), 1) // R
    fields = jnp.where(row_leaf == column_leaf, wide, 0.0).astype(BF16)
    copies[chunks + 2].wait()
    copies[chunks + 3].wait()

    def four_leaves(g, carry):
        local = dot(fields, transfer[:, aligned(g, 4 * R)], NT)
        for j in range(4):
            leaf = g * 4 + j
            total = (local[j * N : (j + 1) * N, :] + far_local[leaf]).astype(BF16)
            out[:, aligned(leaf, LEAF)] = near[:, aligned(leaf, LEAF)] + dot(total, basis[leaf])
        return carry

    lax.fori_loop(0, OWN // 4, four_leaves, 0, unroll=2)


def from_behind(block, axis, distance):
    devices = range(lax.axis_size(axis))
    route = [(i - distance, i) for i in devices if i - distance in devices]
    return lax.ppermute(block, axis, route)


def shards(
    positions, right_sides, leaf_basis, leaf_transfer, far_coupling, top_transfer, top_coupling,
    near_list, send_leaf, send_count, far_target,
):
    both = ("group", "dev")
    points = OWN * LEAF
    rim = EDGE * LEAF
    place = (lax.axis_index("group") * lax.axis_size("dev") + lax.axis_index("dev")).astype(jnp.int32).reshape(1)

    first, last = pl.pallas_call(
        pack_kernel,
        out_shape=(jax.ShapeDtypeStruct((2 * N, rim), BF16),) * 2,
        in_specs=[VMEM, VMEM],
        out_specs=(VMEM, VMEM),
        compiler_params=params(16),
        cost_estimate=pl.CostEstimate(flops=10**7, bytes_accessed=3 << 20, transcendentals=0),
        name="pack",
    )(positions, right_sides)
    below = from_behind(last, both, 1)
    above = from_behind(first, both, -1)

    message = pl.pallas_call(
        moment_kernel,
        out_shape=jax.ShapeDtypeStruct((OWN * 4 * N, 2 * R), BF16),
        in_specs=[SMEM, SMEM, SMEM, VMEM, ANY, VMEM, ANY],
        out_specs=VMEM,
        scratch_shapes=[
            pltpu.VMEM((OWN, R, LEAF), BF16),
            pltpu.VMEM((254, R * R), F32),
            pltpu.VMEM((OWN, N, 2 * R), F32),
            pltpu.VMEM((7, N, 2 * R), F32),
            pltpu.VMEM((6, R, R), F32),
            pltpu.SemaphoreType.DMA((5,)),
        ],
        compiler_params=params(32),
        cost_estimate=pl.CostEstimate(flops=10**9, bytes_accessed=12 << 20, transcendentals=0),
        name="moments",
    )(place, send_leaf[0].T, send_count, right_sides, leaf_basis, leaf_transfer, top_transfer)
    incoming = lax.all_to_all(message, both, split_axis=0, concat_axis=0, tiled=True)

    near = pl.pallas_call(
        near_kernel,
        out_shape=jax.ShapeDtypeStruct((N, points), F32),
        in_specs=[SMEM] + [VMEM] * 4,
        out_specs=VMEM,
        scratch_shapes=[
            pltpu.VMEM((SEEN, LEAF, FEAT), BF16),
            pltpu.VMEM((OWN, FEAT, LEAF), BF16),
            pltpu.VMEM((SEEN, N, LEAF), F32),
        ],
        compiler_params=params(56),
        cost_estimate=pl.CostEstimate(flops=60 * 10**9, bytes_accessed=6 << 20, transcendentals=0),
        name="near",
    )(near_list.T, below, positions, right_sides, above)

    return pl.pallas_call(
        far_kernel,
        out_shape=jax.ShapeDtypeStruct((N, points), F32),
        in_specs=[SMEM, SMEM, VMEM, VMEM, ANY, ANY, ANY, ANY, ANY],
        out_specs=VMEM,
        scratch_shapes=[
            pltpu.VMEM((OWN, R, SLOTS * R), BF16),
            pltpu.VMEM((R, OWN * R), BF16),
            pltpu.VMEM((OWN, R, LEAF), BF16),
            pltpu.VMEM((254, R * R), F32),
            pltpu.VMEM((254, R * R), F32),
            pltpu.VMEM((OWN, N, R), F32),
            pltpu.VMEM((13, R, R), F32),
            pltpu.VMEM((8, N, 2 * R), F32),
            pltpu.SemaphoreType.DMA((8,)),
        ],
        compiler_params=params(56),
        cost_estimate=pl.CostEstimate(flops=2 * 10**9, bytes_accessed=22 << 20, transcendentals=0),
        name="far_field",
    )(place, far_target[0].T, incoming, near, far_coupling[0], leaf_transfer, leaf_basis, top_transfer, top_coupling)


def solution(mesh):
    both = ("group", "dev")
    placed = (
        P(None, both), P(None, both), P(both, None, None), P(None, both), P(both, None, None, None),
        P(), P(), P(both, None), P(both, None, None), P(both, None), P(both, None, None),
    )
    return jax.shard_map(shards, mesh=mesh, in_specs=placed, out_specs=P(None, both), check_vma=False)
```

```python
import functools
import math

import jax
import jax.numpy as jnp
from jax import lax
from jax.experimental import pallas as pl
from jax.experimental.pallas import tpu as pltpu
from jax.sharding import PartitionSpec as P

LEAF = 256
R = 64
N = 8
EDGE = 64
OWN = 128
SEEN = 256
SLOTS = 6
NEAR = 6
FEAT = 32
F32 = jnp.float32
BF16 = jnp.bfloat16

kernel_scale = 0.25 / (4.0 * math.pi)
smoothing = 0.0025
inverse_scale = 1.0 / kernel_scale

NN = (((1,), (0,)), ((), ()))
NT = (((1,), (1,)), ((), ()))
VMEM = pl.BlockSpec(memory_space=pltpu.VMEM)
SMEM = pl.BlockSpec(memory_space=pltpu.SMEM)
ANY = pl.BlockSpec(memory_space=pl.ANY)


def dot(a, b, dims=NN):
    return lax.dot_general(a, b, dims, preferred_element_type=F32)


def exact_dot(a, b, dims=NN):
    return lax.dot_general(a, b, dims, precision=lax.Precision.HIGHEST, preferred_element_type=F32)


def aligned(index, size):
    return pl.ds(pl.multiple_of(index * size, size), size)


def params(megabytes):
    return pltpu.CompilerParams(vmem_limit_bytes=megabytes << 20)


def round16(x):
    return x.astype(BF16).astype(F32)


def split_points(points):
    width = points.shape[1]
    row = lax.broadcasted_iota(jnp.int32, (N, width), 0)
    padded = jnp.concatenate([points, jnp.ones((5, width), F32)], 0)
    x = jnp.where(row < 3, (padded - 1.0) * inverse_scale, 0.0)
    high = round16(x)
    return high + pltpu.roll(round16(x - high), 3, 0)


def square_parts(parts, swapped, offset):
    row = lax.broadcasted_iota(jnp.int32, parts.shape, 0)
    x = jnp.where(row < 3, parts + swapped, 0.0)
    square = jnp.broadcast_to(jnp.sum(x * x, axis=0, keepdims=True), parts.shape) + offset
    s0 = round16(square)
    s1 = round16(square - s0)
    return row, s0, s1, square - s0 - s1


def swap_parts(parts):
    row = lax.broadcasted_iota(jnp.int32, parts.shape, 0)
    return jnp.where(row < 3, pltpu.roll(parts, 5, 0), pltpu.roll(parts, 3, 0))


def source_features(parts):
    row, s0, s1, s2 = square_parts(parts, swap_parts(parts), 0.0)
    first = jnp.where(row < 6, parts, 1.0)
    second = jnp.where(row < 6, parts, jnp.where(row == 6, s0, s1))
    third = jnp.where(row == 0, 1.0, jnp.where(row == 1, s2, 0.0))
    return jnp.concatenate([first, second, third, jnp.zeros_like(parts)], 0).astype(BF16).T


def target_features(parts):
    swapped = swap_parts(parts)
    row, s0, s1, s2 = square_parts(parts, swapped, smoothing * inverse_scale * inverse_scale)
    first = jnp.where(row < 6, -2.0 * parts, jnp.where(row == 6, s0, s1))
    second = jnp.where(row < 6, -2.0 * swapped, 1.0)
    third = jnp.where(row == 0, s2, jnp.where(row == 1, 1.0, 0.0))
    return jnp.concatenate([first, second, third, jnp.zeros_like(parts)], 0).astype(BF16)


def inverse_root(distance):
    return lax.rsqrt(distance).astype(BF16)


def pack_kernel(points_hbm, values_hbm, first, last, points, values, sems):
    chunks = 4
    width = OWN * LEAF // chunks
    copies = []
    for i in range(chunks):
        some = pl.ds(i * width, width)
        copies.append(pltpu.make_async_copy(points_hbm.at[:, some], points.at[:, some], sems.at[2 * i]))
        copies.append(pltpu.make_async_copy(values_hbm.at[:, some], values.at[:, some], sems.at[2 * i + 1]))
    for copy in copies:
        copy.start()
    for i in range(chunks):
        copies[2 * i].wait()
        copies[2 * i + 1].wait()
        for j in range(i * width, (i + 1) * width, 4 * LEAF):
            some = slice(j, j + 4 * LEAF)
            out, start = (first, j) if j < EDGE * LEAF else (last, j - EDGE * LEAF)
            rows = jnp.concatenate([values[:, some], split_points(points[:, some])], 0)
            out[:, start : start + 4 * LEAF] = rows.astype(BF16)


def top_bit(x):
    return jnp.maximum(31 - lax.clz(x), 0)


def node_of(owner, level):
    return 2 * OWN - 2 * (OWN >> level) + lax.shift_right_logical(owner, level)


def path_copies(table, rows, owner, sems, first):
    copies = []
    for level in range(5):
        start = pl.multiple_of(lax.shift_right_logical(node_of(owner, level), 3) * 8, 8)
        copies.append(pltpu.make_async_copy(table.at[pl.ds(start, 8)], rows.at[level], sems.at[first + level]))
    copies.append(pltpu.make_async_copy(table.at[pl.ds(248, 6)], rows.at[5, pl.ds(0, 6)], sems.at[first + 5]))
    return copies


def path_matrix(rows, owner, level, matrices, slot):
    node = node_of(owner, level)
    fetch(rows.at[min(level, 5)], lax.bitwise_and(node, 7), matrices, slot)


def moment_kernel(
    place, send_leaf, send_count, values_hbm, basis_hbm, transfer_hbm, top_transfer_hbm,
    message, values, basis, transfer, rows, moments, chain, matrices, sems,
):
    owner = place[0]
    chunks = 4
    chunk = OWN // chunks
    copies = []
    for i in range(chunks):
        some = pl.ds(i * chunk * LEAF, chunk * LEAF)
        copies.append(pltpu.make_async_copy(values_hbm.at[:, some], values.at[:, some], sems.at[3 * i]))
        some = pl.ds(i * chunk, chunk)
        copies.append(pltpu.make_async_copy(basis_hbm.at[some], basis.at[some], sems.at[3 * i + 1]))
        some = pl.ds(i * chunk * R, chunk * R)
        copies.append(pltpu.make_async_copy(transfer_hbm.at[:, some], transfer.at[:, some], sems.at[3 * i + 2]))
    paths = path_copies(top_transfer_hbm, rows, owner, sems, 3 * chunks)
    for copy in copies + paths:
        copy.start()

    def some_leaves(g, total):
        picked = []
        for j in range(16):
            leaf = g * 16 + j
            v = values[:, aligned(leaf, LEAF)].astype(BF16)
            picked.append(round16(dot(v, basis[leaf], NT)))
        for j in range(16):
            moments[g * 16 + j] = jnp.concatenate([picked[j], picked[j]], 1)
        for j in range(0, 16, 4):
            four = jnp.concatenate(picked[j : j + 4], 0).astype(BF16)
            total = total + dot(four, transfer[:, aligned(g * 4 + j // 4, 4 * R)])
        return total

    total = jnp.zeros((4 * N, 4 * R), F32)
    for i in range(chunks):
        for copy in copies[3 * i : 3 * i + 3]:
            copy.wait()
        total = lax.fori_loop(i * chunk // 16, (i + 1) * chunk // 16, some_leaves, total)
    current = total[0:N, 0:R]
    for j in range(1, 4):
        current = current + total[j * N : (j + 1) * N, j * R : (j + 1) * R]
    current = current * (1.0 / math.sqrt(OWN))

    for copy in paths:
        copy.wait()
    for level in range(6):
        path_matrix(rows, owner, level, matrices, level)
    for level in range(7):
        high = round16(current)
        chain[level] = jnp.concatenate([high, current - high], 1)
        if level < 6:
            current = exact_dot(current, matrices[level])

    is_left = lax.broadcasted_iota(jnp.int32, (N, 2 * R), 1) < R

    def one_receiver(p, carry):
        parts = []
        count = send_count[0, p]
        for pair in range(SLOTS // 2):
            left = moments[send_leaf[2 * pair, p]]
            right = moments[send_leaf[2 * pair + 1, p]]
            left = jnp.where(2 * pair < count, left, 0.0)
            right = jnp.where(2 * pair + 1 < count, right, 0.0)
            parts.append(jnp.where(is_left, left, right))
        parts.append(chain[top_bit(owner ^ p)])
        message[aligned(p, 4 * N), :] = jnp.concatenate(parts, 0).astype(BF16)
        return carry

    lax.fori_loop(0, OWN, one_receiver, 0, unroll=8)


def near_kernel(
    near_list, below, points, values, above, out, sources, targets, seen_values,
):
    def rim(ref, first):
        def one(i, carry):
            block = ref[:, aligned(i, LEAF)].astype(F32)
            sources[first + i] = source_features(block[N:, :])
            seen_values[first + i] = block[:N, :]
            return carry

        lax.fori_loop(0, EDGE, one, 0, unroll=4)

    def own(i, carry):
        parts = split_points(points[:, aligned(i, LEAF)])
        sources[EDGE + i] = source_features(parts)
        targets[i] = target_features(parts)
        seen_values[EDGE + i] = values[:, aligned(i, LEAF)]
        return carry

    lax.fori_loop(0, OWN, own, 0, unroll=4)
    rim(below, 0)
    rim(above, EDGE + OWN)

    def finish(leaf, seen, kernels):
        total = dot(seen_values[seen[0]].astype(BF16), kernels[0])
        for e, kernel in zip(seen[1:], kernels[1:]):
            total = total + dot(seen_values[e].astype(BF16), kernel)
        out[:, aligned(leaf, LEAF)] = total

    def eight_leaves(g, carry):
        waiting = None
        for j in range(8):
            leaf = g * 8 + j
            target = targets[leaf]
            seen = [EDGE + leaf] + [near_list[k, leaf] for k in range(NEAR)]
            kernels = [inverse_root(dot(sources[e], target)) for e in seen]
            if waiting is not None:
                finish(*waiting)
            waiting = (leaf, seen, kernels)
        finish(*waiting)
        return carry

    lax.fori_loop(0, OWN // 8, eight_leaves, 0)


def fetch(table, row, matrices, slot):
    flat = table[pl.ds(row, 1), :]
    for j in range(R // 2):
        pair = flat[:, j * 2 * R : (j + 1) * 2 * R]
        matrices[slot, 2 * j : 2 * j + 1, 0:R] = pair[:, 0:R]
        matrices[slot, 2 * j + 1 : 2 * j + 2, 0:R] = pair[:, R : 2 * R]


def far_kernel(
    place, far_target, incoming, near,
    coupling_hbm, transfer_hbm, basis_hbm, top_transfer_hbm, top_coupling_hbm,
    out,
    coupling, transfer, basis, transfer_rows, coupling_rows, far_local, matrices, siblings, sems,
):
    owner = place[0]
    chunks = 4
    chunk = OWN // chunks
    copies = []
    for i in range(chunks):
        copies.append(pltpu.make_async_copy(coupling_hbm.at[pl.ds(i * chunk, chunk)], coupling.at[pl.ds(i * chunk, chunk)], sems.at[i]))
    copies.append(pltpu.make_async_copy(transfer_hbm, transfer, sems.at[chunks]))
    copies.append(pltpu.make_async_copy(basis_hbm, basis, sems.at[chunks + 1]))
    paths = path_copies(top_transfer_hbm, transfer_rows, owner, sems, chunks + 2)
    paths = paths + path_copies(top_coupling_hbm, coupling_rows, owner, sems, chunks + 8)
    for copy in copies[:chunks] + paths + copies[chunks:]:
        copy.start()

    far_local[...] = jnp.zeros_like(far_local)
    siblings[...] = jnp.zeros_like(siblings)
    is_left = lax.broadcasted_iota(jnp.int32, (N, 2 * R), 1) < R

    for i in range(chunks):
        copies[i].wait()

        def two_senders(g, carry):
            arrived = incoming[aligned(g, 64), :].astype(F32)
            results = []
            for j in range(2):
                p = g * 2 + j
                for pair in range(SLOTS // 2):
                    tile = arrived[(j * 4 + pair) * N : (j * 4 + pair + 1) * N, :]
                    left = jnp.where(is_left, tile, 0.0)
                    right = jnp.where(is_left, 0.0, tile)
                    both = jnp.concatenate([left, right], 0).astype(BF16)
                    matrix = coupling[p, :, pair * 2 * R : (pair + 1) * 2 * R]
                    results.append(dot(both, matrix, NT))
            for j in range(2):
                p = g * 2 + j
                level = jnp.where(p == owner, 7, top_bit(owner ^ p))
                siblings[level] = siblings[level] + arrived[(j * 4 + 3) * N : (j * 4 + 4) * N, :]
                for slot in range(SLOTS):
                    leaf = far_target[slot, p]
                    part = results[j * 3 + slot // 2][(slot % 2) * N : (slot % 2 + 1) * N, :]
                    far_local[leaf] = far_local[leaf] + part
            return carry

        lax.fori_loop(i * chunk // 2, (i + 1) * chunk // 2, two_senders, 0, unroll=4)

    for copy in paths:
        copy.wait()
    for level in range(7):
        path_matrix(coupling_rows, owner, level, matrices, level)
        if level < 6:
            path_matrix(transfer_rows, owner, level, matrices, 7 + level)
    coupled = []
    for level in range(7):
        both = siblings[level]
        coupled.append(exact_dot(both[:, :R] + both[:, R:], matrices[level], NT))
    field = coupled[6]
    for level in reversed(range(6)):
        field = coupled[level] + exact_dot(field, matrices[7 + level], NT)
    field = round16(field)

    wide = jnp.concatenate([jnp.concatenate([field] * 4, 1)] * 4, 0)
    row_leaf = lax.broadcasted_iota(jnp.int32, (4 * N, 4 * R), 0) // N
    column_leaf = lax.broadcasted_iota(jnp.int32, (4 * N, 4 * R), 1) // R
    fields = jnp.where(row_leaf == column_leaf, wide, 0.0).astype(BF16)
    copies[chunks].wait()
    copies[chunks + 1].wait()

    def some_leaves(g, carry):
        locals_ = []
        for i in range(4):
            locals_.append(dot(fields, transfer[:, aligned(g * 4 + i, 4 * R)], NT))
        for j in range(16):
            leaf = g * 16 + j
            total = (locals_[j // 4][(j % 4) * N : (j % 4 + 1) * N, :] + far_local[leaf]).astype(BF16)
            out[:, aligned(leaf, LEAF)] = near[:, aligned(leaf, LEAF)] + dot(total, basis[leaf])
        return carry

    lax.fori_loop(0, OWN // 16, some_leaves, 0)


def from_behind(block, axis, distance):
    devices = range(lax.axis_size(axis))
    route = [(i - distance, i) for i in devices if i - distance in devices]
    return lax.ppermute(block, axis, route)


def shards(
    positions, right_sides, leaf_basis, leaf_transfer, far_coupling, top_transfer, top_coupling,
    near_list, send_leaf, send_count, far_target,
):
    both = ("group", "dev")
    points = OWN * LEAF
    rim = EDGE * LEAF
    place = (lax.axis_index("group") * lax.axis_size("dev") + lax.axis_index("dev")).astype(jnp.int32).reshape(1)

    first, last = pl.pallas_call(
        pack_kernel,
        out_shape=(jax.ShapeDtypeStruct((2 * N, rim), BF16),) * 2,
        in_specs=[ANY, ANY],
        out_specs=(VMEM, VMEM),
        scratch_shapes=[pltpu.VMEM((3, points), F32), pltpu.VMEM((N, points), F32), pltpu.SemaphoreType.DMA((8,))],
        compiler_params=params(60),
        cost_estimate=pl.CostEstimate(flops=10**7, bytes_accessed=3 << 20, transcendentals=0),
        name="pack",
    )(positions, right_sides)
    below = from_behind(last, both, 1)
    above = from_behind(first, both, -1)

    message = pl.pallas_call(
        moment_kernel,
        out_shape=jax.ShapeDtypeStruct((OWN * 4 * N, 2 * R), BF16),
        in_specs=[SMEM, SMEM, SMEM, ANY, ANY, ANY, ANY],
        out_specs=VMEM,
        scratch_shapes=[
            pltpu.VMEM((N, points), F32),
            pltpu.VMEM((OWN, R, LEAF), BF16),
            pltpu.VMEM((R, OWN * R), BF16),
            pltpu.VMEM((6, 8, R * R), F32),
            pltpu.VMEM((OWN, N, 2 * R), F32),
            pltpu.VMEM((7, N, 2 * R), F32),
            pltpu.VMEM((6, R, R), F32),
            pltpu.SemaphoreType.DMA((18,)),
        ],
        compiler_params=params(60),
        cost_estimate=pl.CostEstimate(flops=10**9, bytes_accessed=12 << 20, transcendentals=0),
        name="moments",
    )(place, send_leaf[0].T, send_count, right_sides, leaf_basis, leaf_transfer, top_transfer)
    incoming = lax.all_to_all(message, both, split_axis=0, concat_axis=0, tiled=True)

    near = pl.pallas_call(
        near_kernel,
        out_shape=jax.ShapeDtypeStruct((N, points), F32),
        in_specs=[SMEM] + [VMEM] * 4,
        out_specs=VMEM,
        scratch_shapes=[
            pltpu.VMEM((SEEN, LEAF, FEAT), BF16),
            pltpu.VMEM((OWN, FEAT, LEAF), BF16),
            pltpu.VMEM((SEEN, N, LEAF), F32),
        ],
        compiler_params=params(56),
        cost_estimate=pl.CostEstimate(flops=60 * 10**9, bytes_accessed=6 << 20, transcendentals=0),
        name="near",
    )(near_list.T, below, positions, right_sides, above)

    return pl.pallas_call(
        far_kernel,
        out_shape=jax.ShapeDtypeStruct((N, points), F32),
        in_specs=[SMEM, SMEM, VMEM, VMEM, ANY, ANY, ANY, ANY, ANY],
        out_specs=VMEM,
        scratch_shapes=[
            pltpu.VMEM((OWN, R, SLOTS * R), BF16),
            pltpu.VMEM((R, OWN * R), BF16),
            pltpu.VMEM((OWN, R, LEAF), BF16),
            pltpu.VMEM((6, 8, R * R), F32),
            pltpu.VMEM((6, 8, R * R), F32),
            pltpu.VMEM((OWN, N, R), F32),
            pltpu.VMEM((13, R, R), F32),
            pltpu.VMEM((8, N, 2 * R), F32),
            pltpu.SemaphoreType.DMA((18,)),
        ],
        compiler_params=params(56),
        cost_estimate=pl.CostEstimate(flops=2 * 10**9, bytes_accessed=22 << 20, transcendentals=0),
        name="far_field",
    )(place, far_target[0].T, incoming, near, far_coupling[0], leaf_transfer, leaf_basis, top_transfer, top_coupling)


def solution(mesh):
    both = ("group", "dev")
    placed = (
        P(None, both), P(None, both), P(both, None, None), P(None, both), P(both, None, None, None),
        P(), P(), P(both, None), P(both, None, None), P(both, None), P(both, None, None),
    )
    return jax.shard_map(shards, mesh=mesh, in_specs=placed, out_specs=P(None, both), check_vma=False)
```

```python
import functools
import math

import jax
import jax.numpy as jnp
from jax import lax
from jax.experimental import pallas as pl
from jax.experimental.pallas import tpu as pltpu
from jax.sharding import PartitionSpec as P

LEAF = 256
R = 64
N = 8
EDGE = 64
OWN = 128
SEEN = 256
SLOTS = 6
NEAR = 6
FEAT = 32
F32 = jnp.float32
BF16 = jnp.bfloat16

kernel_scale = 0.25 / (4.0 * math.pi)
smoothing = 0.0025
inverse_scale = 1.0 / kernel_scale

NN = (((1,), (0,)), ((), ()))
NT = (((1,), (1,)), ((), ()))
VMEM = pl.BlockSpec(memory_space=pltpu.VMEM)
SMEM = pl.BlockSpec(memory_space=pltpu.SMEM)
HBM = pl.BlockSpec(memory_space=pltpu.HBM)


def dot(a, b, dims=NN):
    return lax.dot_general(a, b, dims, preferred_element_type=F32)


def exact_dot(a, b, dims=NN):
    return lax.dot_general(a, b, dims, precision=lax.Precision.HIGHEST, preferred_element_type=F32)


def aligned(index, size):
    return pl.ds(pl.multiple_of(index * size, size), size)


def params(megabytes):
    return pltpu.CompilerParams(vmem_limit_bytes=megabytes << 20)


def round16(x):
    return x.astype(BF16).astype(F32)


def split_points(points):
    width = points.shape[1]
    row = lax.broadcasted_iota(jnp.int32, (N, width), 0)
    padded = jnp.concatenate([points, jnp.ones((5, width), F32)], 0)
    x = jnp.where(row < 3, (padded - 1.0) * inverse_scale, 0.0)
    high = round16(x)
    return high + pltpu.roll(round16(x - high), 3, 0)


def square_parts(parts, swapped, offset):
    row = lax.broadcasted_iota(jnp.int32, parts.shape, 0)
    x = jnp.where(row < 3, parts + swapped, 0.0)
    square = jnp.broadcast_to(jnp.sum(x * x, axis=0, keepdims=True), parts.shape) + offset
    s0 = round16(square)
    s1 = round16(square - s0)
    return row, s0, s1, square - s0 - s1


def swap_parts(parts):
    row = lax.broadcasted_iota(jnp.int32, parts.shape, 0)
    return jnp.where(row < 3, pltpu.roll(parts, 5, 0), pltpu.roll(parts, 3, 0))


def source_features(parts):
    row, s0, s1, s2 = square_parts(parts, swap_parts(parts), 0.0)
    first = jnp.where(row < 6, parts, 1.0)
    second = jnp.where(row < 6, parts, jnp.where(row == 6, s0, s1))
    third = jnp.where(row == 0, 1.0, jnp.where(row == 1, s2, 0.0))
    return jnp.concatenate([first, second, third, jnp.zeros_like(parts)], 0).astype(BF16).T


def target_features(parts):
    swapped = swap_parts(parts)
    row, s0, s1, s2 = square_parts(parts, swapped, smoothing * inverse_scale * inverse_scale)
    first = jnp.where(row < 6, -2.0 * parts, jnp.where(row == 6, s0, s1))
    second = jnp.where(row < 6, -2.0 * swapped, 1.0)
    third = jnp.where(row == 0, s2, jnp.where(row == 1, 1.0, 0.0))
    return jnp.concatenate([first, second, third, jnp.zeros_like(parts)], 0).astype(BF16)


def inverse_root(distance):
    return lax.rsqrt(distance).astype(BF16)


def pack_kernel(place, points_hbm, values_hbm, first, second, points, values, sems):
    copies = [
        pltpu.make_async_copy(points_hbm, points, sems.at[0]),
        pltpu.make_async_copy(values_hbm, values, sems.at[1]),
    ]
    for copy in copies:
        copy.start()
    for copy in copies:
        copy.wait()
    odd = lax.bitwise_and(place[0], 1)
    width = 4 * LEAF
    for out, side in ((first, 1 - odd), (second, odd)):
        for j in range(EDGE // 4):
            some = aligned(side * (EDGE // 4) + j, width)
            rows = jnp.concatenate([values[:, some], split_points(points[:, some])], 0)
            out[:, j * width : (j + 1) * width] = rows.astype(BF16)


def top_bit(x):
    return jnp.maximum(31 - lax.clz(x), 0)


def node_of(owner, level):
    return 2 * OWN - 2 * (OWN >> level) + lax.shift_right_logical(owner, level)


def path_copies(table, rows, owner, sems, first):
    copies = []
    for level in range(5):
        start = pl.multiple_of(lax.shift_right_logical(node_of(owner, level), 3) * 8, 8)
        copies.append(pltpu.make_async_copy(table.at[pl.ds(start, 8)], rows.at[level], sems.at[first + level]))
    copies.append(pltpu.make_async_copy(table.at[pl.ds(248, 6)], rows.at[5, pl.ds(0, 6)], sems.at[first + 5]))
    return copies


def path_matrix(rows, owner, level, matrices, slot):
    node = node_of(owner, level)
    fetch(rows.at[min(level, 5)], lax.bitwise_and(node, 7), matrices, slot)


def moment_kernel(
    place, send_leaf, send_count, values_hbm, basis_hbm, transfer_hbm, top_transfer_hbm,
    message, values, basis, transfer, rows, moments, chain, matrices, sems,
):
    owner = place[0]
    chunks = 4
    chunk = OWN // chunks
    copies = []
    for i in range(chunks):
        some = pl.ds(i * chunk * LEAF, chunk * LEAF)
        copies.append(pltpu.make_async_copy(values_hbm.at[:, some], values.at[:, some], sems.at[3 * i]))
        some = pl.ds(i * chunk, chunk)
        copies.append(pltpu.make_async_copy(basis_hbm.at[some], basis.at[some], sems.at[3 * i + 1]))
        some = pl.ds(i * chunk * R, chunk * R)
        copies.append(pltpu.make_async_copy(transfer_hbm.at[:, some], transfer.at[:, some], sems.at[3 * i + 2]))
    paths = path_copies(top_transfer_hbm, rows, owner, sems, 3 * chunks)
    for copy in copies + paths:
        copy.start()

    def some_leaves(g, total):
        picked = []
        for j in range(16):
            leaf = g * 16 + j
            v = values[:, aligned(leaf, LEAF)].astype(BF16)
            picked.append(round16(dot(v, basis[leaf], NT)))
        for j in range(16):
            moments[g * 16 + j] = jnp.concatenate([picked[j], picked[j]], 1)
        for j in range(0, 16, 4):
            four = jnp.concatenate(picked[j : j + 4], 0).astype(BF16)
            total = total + dot(four, transfer[:, aligned(g * 4 + j // 4, 4 * R)])
        return total

    total = jnp.zeros((4 * N, 4 * R), F32)
    for i in range(chunks):
        for copy in copies[3 * i : 3 * i + 3]:
            copy.wait()
        total = lax.fori_loop(i * chunk // 16, (i + 1) * chunk // 16, some_leaves, total)
    current = total[0:N, 0:R]
    for j in range(1, 4):
        current = current + total[j * N : (j + 1) * N, j * R : (j + 1) * R]
    current = current * (1.0 / math.sqrt(OWN))

    for copy in paths:
        copy.wait()
    for level in range(6):
        path_matrix(rows, owner, level, matrices, level)
    for level in range(7):
        high = round16(current)
        chain[level] = jnp.concatenate([high, current - high], 1)
        if level < 6:
            current = exact_dot(current, matrices[level])

    is_left = lax.broadcasted_iota(jnp.int32, (N, 2 * R), 1) < R

    def one_receiver(p, carry):
        parts = []
        count = send_count[0, p]
        for pair in range(SLOTS // 2):
            left = moments[send_leaf[2 * pair, 0, p]]
            right = moments[send_leaf[2 * pair + 1, 0, p]]
            left = jnp.where(2 * pair < count, left, 0.0)
            right = jnp.where(2 * pair + 1 < count, right, 0.0)
            parts.append(jnp.where(is_left, left, right))
        parts.append(chain[top_bit(owner ^ p)])
        message[aligned(p, 4 * N), :] = jnp.concatenate(parts, 0).astype(BF16)
        return carry

    lax.fori_loop(0, OWN, one_receiver, 0, unroll=8)


def near_kernel(
    place, near_list, first, second, points_hbm, values_hbm, out, points, values, sources, targets, seen_values, sems,
):
    copies = [
        pltpu.make_async_copy(points_hbm, points, sems.at[0]),
        pltpu.make_async_copy(values_hbm, values, sems.at[1]),
    ]
    for copy in copies:
        copy.start()
    odd = lax.bitwise_and(place[0], 1)

    def rim(ref, start):
        def one(i, carry):
            block = ref[:, aligned(i, LEAF)].astype(F32)
            sources[start + i] = source_features(block[N:, :])
            seen_values[start + i] = block[:N, :]
            return carry

        lax.fori_loop(0, EDGE, one, 0, unroll=4)

    def own(i, carry):
        parts = split_points(points[:, aligned(i, LEAF)])
        sources[EDGE + i] = source_features(parts)
        targets[i] = target_features(parts)
        seen_values[EDGE + i] = values[:, aligned(i, LEAF)]
        return carry

    rim(first, (1 - odd) * (EDGE + OWN))
    rim(second, odd * (EDGE + OWN))
    for copy in copies:
        copy.wait()
    lax.fori_loop(0, OWN, own, 0, unroll=4)

    def eight_leaves(g, carry):
        pairs = []
        for j in range(8):
            leaf = g * 8 + j
            seen = [EDGE + leaf] + [near_list[k, leaf] for k in range(NEAR)]
            pairs.extend((leaf, (j, k), e) for k, e in enumerate(seen))
        groups = [pairs[i : i + 8] for i in range(0, len(pairs), 8)]
        kernels = {}
        total = None
        for ahead, now in zip(groups + [[]], [[]] + groups):
            for i in range(0, 8, 4):
                for leaf, pair, e in ahead[i : i + 4]:
                    kernels[pair] = inverse_root(dot(sources[e], targets[leaf]))
                for leaf, pair, e in now[i : i + 4]:
                    part = dot(seen_values[e].astype(BF16), kernels.pop(pair))
                    total = part if pair[1] == 0 else total + part
                    if pair[1] == NEAR:
                        out[:, aligned(leaf, LEAF)] = total
        return carry

    lax.fori_loop(0, OWN // 8, eight_leaves, 0)


def fetch(table, row, matrices, slot):
    flat = table[pl.ds(row, 1), :]
    for j in range(R // 2):
        pair = flat[:, j * 2 * R : (j + 1) * 2 * R]
        matrices[slot, 2 * j : 2 * j + 1, 0:R] = pair[:, 0:R]
        matrices[slot, 2 * j + 1 : 2 * j + 2, 0:R] = pair[:, R : 2 * R]


def far_kernel(
    place, far_target, incoming, near_hbm,
    coupling_hbm, transfer_hbm, basis_hbm, top_transfer_hbm, top_coupling_hbm,
    out_hbm,
    near, out, coupling, transfer, basis, transfer_rows, coupling_rows, far_local, matrices, siblings, sems,
):
    owner = place[0]
    chunks = 4
    chunk = OWN // chunks
    copies = []
    for i in range(chunks):
        some = pl.ds(i * chunk, chunk)
        copies.append(pltpu.make_async_copy(coupling_hbm.at[some], coupling.at[some], sems.at[i]))
    paths = path_copies(top_transfer_hbm, transfer_rows, owner, sems, chunks)
    paths = paths + path_copies(top_coupling_hbm, coupling_rows, owner, sems, chunks + 6)
    first = chunks + 12
    rest = [
        pltpu.make_async_copy(source, target, sems.at[first + i])
        for i, (source, target) in enumerate([(transfer_hbm, transfer), (basis_hbm, basis), (near_hbm, near)])
    ]
    for copy in copies + paths + rest:
        copy.start()

    far_local[...] = jnp.zeros_like(far_local)
    siblings[...] = jnp.zeros_like(siblings)
    is_left = lax.broadcasted_iota(jnp.int32, (N, 2 * R), 1) < R

    for i in range(chunks):
        copies[i].wait()

        def two_senders(g, carry):
            arrived = incoming[aligned(g, 64), :].astype(F32)
            results = []
            for j in range(2):
                p = g * 2 + j
                for pair in range(SLOTS // 2):
                    tile = arrived[(j * 4 + pair) * N : (j * 4 + pair + 1) * N, :]
                    left = jnp.where(is_left, tile, 0.0)
                    right = jnp.where(is_left, 0.0, tile)
                    both = jnp.concatenate([left, right], 0).astype(BF16)
                    matrix = coupling[p, :, pair * 2 * R : (pair + 1) * 2 * R]
                    results.append(dot(both, matrix, NT))
            for j in range(2):
                p = g * 2 + j
                level = jnp.where(p == owner, 7, top_bit(owner ^ p))
                siblings[level] = siblings[level] + arrived[(j * 4 + 3) * N : (j * 4 + 4) * N, :]
                for slot in range(SLOTS):
                    leaf = far_target[slot, 0, p]
                    part = results[j * 3 + slot // 2][(slot % 2) * N : (slot % 2 + 1) * N, :]
                    far_local[leaf] = far_local[leaf] + part
            return carry

        lax.fori_loop(i * chunk // 2, (i + 1) * chunk // 2, two_senders, 0, unroll=4)

    for copy in paths:
        copy.wait()
    for level in range(7):
        path_matrix(coupling_rows, owner, level, matrices, level)
        if level < 6:
            path_matrix(transfer_rows, owner, level, matrices, 7 + level)
    coupled = []
    for level in range(7):
        both = siblings[level]
        coupled.append(exact_dot(both[:, :R] + both[:, R:], matrices[level], NT))
    field = coupled[6]
    for level in reversed(range(6)):
        field = coupled[level] + exact_dot(field, matrices[7 + level], NT)
    field = round16(field)

    wide = jnp.concatenate([jnp.concatenate([field] * 4, 1)] * 4, 0)
    row_leaf = lax.broadcasted_iota(jnp.int32, (4 * N, 4 * R), 0) // N
    column_leaf = lax.broadcasted_iota(jnp.int32, (4 * N, 4 * R), 1) // R
    fields = jnp.where(row_leaf == column_leaf, wide, 0.0).astype(BF16)
    for copy in rest:
        copy.wait()

    def some_leaves(g, carry):
        locals_ = []
        for i in range(4):
            locals_.append(dot(fields, transfer[:, aligned(g * 4 + i, 4 * R)], NT))
        for j in range(16):
            leaf = g * 16 + j
            total = (locals_[j // 4][(j % 4) * N : (j % 4 + 1) * N, :] + far_local[leaf]).astype(BF16)
            out[:, aligned(leaf, LEAF)] = near[:, aligned(leaf, LEAF)] + dot(total, basis[leaf])
        return carry

    results = []
    for i in range(chunks):
        lax.fori_loop(i * chunk // 16, (i + 1) * chunk // 16, some_leaves, 0)
        some = pl.ds(i * chunk * LEAF, chunk * LEAF)
        results.append(pltpu.make_async_copy(out.at[:, some], out_hbm.at[:, some], sems.at[first + 3 + i]))
        results[-1].start()
    for copy in results:
        copy.wait()


def swapped(block, axis, start):
    lower = range(start, lax.axis_size(axis) - 1, 2)
    return lax.ppermute(block, axis, [(i, i + 1) for i in lower] + [(i + 1, i) for i in lower])


def shards(
    positions, right_sides, leaf_basis, leaf_transfer, far_coupling, top_transfer, top_coupling,
    near_list, send_leaf, send_count, far_target,
):
    both = ("group", "dev")
    points = OWN * LEAF
    rim = EDGE * LEAF
    place = (lax.axis_index("group") * lax.axis_size("dev") + lax.axis_index("dev")).astype(jnp.int32).reshape(1)

    first, second = pl.pallas_call(
        pack_kernel,
        out_shape=(jax.ShapeDtypeStruct((2 * N, rim), BF16),) * 2,
        in_specs=[SMEM, HBM, HBM],
        out_specs=(VMEM, VMEM),
        scratch_shapes=[pltpu.VMEM((3, points), F32), pltpu.VMEM((N, points), F32), pltpu.SemaphoreType.DMA((2,))],
        compiler_params=params(63),
        cost_estimate=pl.CostEstimate(flops=10**7, bytes_accessed=3 << 20, transcendentals=0),
        name="pack",
    )(place, positions, right_sides)
    first = swapped(first, both, 0)
    second = swapped(second, both, 1)

    message = pl.pallas_call(
        moment_kernel,
        out_shape=jax.ShapeDtypeStruct((OWN * 4 * N, 2 * R), BF16),
        in_specs=[SMEM, SMEM, SMEM, HBM, HBM, HBM, HBM],
        out_specs=VMEM,
        scratch_shapes=[
            pltpu.VMEM((N, points), F32),
            pltpu.VMEM((OWN, R, LEAF), BF16),
            pltpu.VMEM((R, OWN * R), BF16),
            pltpu.VMEM((6, 8, R * R), F32),
            pltpu.VMEM((OWN, N, 2 * R), F32),
            pltpu.VMEM((7, N, 2 * R), F32),
            pltpu.VMEM((6, R, R), F32),
            pltpu.SemaphoreType.DMA((18,)),
        ],
        compiler_params=params(63),
        cost_estimate=pl.CostEstimate(flops=10**9, bytes_accessed=12 << 20, transcendentals=0),
        name="moments",
    )(place, send_leaf.transpose(2, 0, 1), send_count, right_sides, leaf_basis, leaf_transfer, top_transfer)
    incoming = lax.all_to_all(message, both, split_axis=0, concat_axis=0, tiled=True)

    near = pl.pallas_call(
        near_kernel,
        out_shape=jax.ShapeDtypeStruct((N, points), F32),
        in_specs=[SMEM, SMEM, VMEM, VMEM, HBM, HBM],
        out_specs=VMEM,
        scratch_shapes=[
            pltpu.VMEM((3, points), F32),
            pltpu.VMEM((N, points), F32),
            pltpu.VMEM((SEEN, LEAF, FEAT), BF16),
            pltpu.VMEM((OWN, FEAT, LEAF), BF16),
            pltpu.VMEM((SEEN, N, LEAF), F32),
            pltpu.SemaphoreType.DMA((2,)),
        ],
        compiler_params=params(63),
        cost_estimate=pl.CostEstimate(flops=60 * 10**9, bytes_accessed=6 << 20, transcendentals=0),
        name="near",
    )(place, near_list.T, first, second, positions, right_sides)

    return pl.pallas_call(
        far_kernel,
        out_shape=jax.ShapeDtypeStruct((N, points), F32),
        in_specs=[SMEM, SMEM, VMEM] + [HBM] * 6,
        out_specs=HBM,
        scratch_shapes=[
            pltpu.VMEM((N, points), F32),
            pltpu.VMEM((N, points), F32),
            pltpu.VMEM((OWN, R, SLOTS * R), BF16),
            pltpu.VMEM((R, OWN * R), BF16),
            pltpu.VMEM((OWN, R, LEAF), BF16),
            pltpu.VMEM((6, 8, R * R), F32),
            pltpu.VMEM((6, 8, R * R), F32),
            pltpu.VMEM((OWN, N, R), F32),
            pltpu.VMEM((13, R, R), F32),
            pltpu.VMEM((8, N, 2 * R), F32),
            pltpu.SemaphoreType.DMA((23,)),
        ],
        compiler_params=params(63),
        cost_estimate=pl.CostEstimate(flops=2 * 10**9, bytes_accessed=22 << 20, transcendentals=0),
        name="far_field",
    )(place, far_target.transpose(2, 0, 1), incoming, near, far_coupling[0], leaf_transfer, leaf_basis, top_transfer, top_coupling)


def solution(mesh):
    both = ("group", "dev")
    placed = (
        P(None, both), P(None, both), P(both, None, None), P(None, both), P(both, None, None, None),
        P(), P(), P(both, None), P(both, None, None), P(both, None), P(both, None, None),
    )
    return jax.shard_map(shards, mesh=mesh, in_specs=placed, out_specs=P(None, both), check_vma=False)
```

```python
import functools
import math

import jax
import jax.numpy as jnp
import numpy as np
from jax import lax
from jax.experimental import pallas as pl
from jax.experimental.pallas import tpu as pltpu
from jax.sharding import PartitionSpec as P

LEAF = 256
R = 64
N = 8
EDGE = 64
OWN = 128
SEEN = 256
SLOTS = 6
NEAR = 6
FEAT = 32
F32 = jnp.float32
BF16 = jnp.bfloat16

kernel_scale = 0.25 / (4.0 * math.pi)
smoothing = 0.0025
inverse_scale = 1.0 / kernel_scale

NN = (((1,), (0,)), ((), ()))
NT = (((1,), (1,)), ((), ()))
VMEM = pl.BlockSpec(memory_space=pltpu.VMEM)
SMEM = pl.BlockSpec(memory_space=pltpu.SMEM)
HBM = pl.BlockSpec(memory_space=pltpu.HBM)


def dot(a, b, dims=NN):
    return lax.dot_general(a, b, dims, preferred_element_type=F32)


def exact_dot(a, b, dims=NN):
    return lax.dot_general(a, b, dims, precision=lax.Precision.HIGHEST, preferred_element_type=F32)


def aligned(index, size):
    return pl.ds(pl.multiple_of(index * size, size), size)


def params(megabytes):
    return pltpu.CompilerParams(vmem_limit_bytes=megabytes << 20)


def round16(x):
    return x.astype(BF16).astype(F32)


def split_points(points):
    width = points.shape[1]
    row = lax.broadcasted_iota(jnp.int32, (N, width), 0)
    padded = jnp.concatenate([points, jnp.ones((5, width), F32)], 0)
    x = jnp.where(row < 3, (padded - 1.0) * inverse_scale, 0.0)
    high = round16(x)
    return high + pltpu.roll(round16(x - high), 3, 0)


def features(parts):
    row = lax.broadcasted_iota(jnp.int32, parts.shape, 0)
    swapped = jnp.where(row < 3, pltpu.roll(parts, 5, 0), pltpu.roll(parts, 3, 0))
    x = jnp.where(row < 3, parts + swapped, 0.0)
    square = x * x
    for shift in (4, 2, 1):
        square = square + pltpu.roll(square, shift, 0)
    s0 = round16(square)
    rest = square - s0
    s1 = round16(rest)
    s2 = rest - s1
    squares = jnp.where(row == 6, s0, s1)
    zero = jnp.zeros_like(parts)
    offset = smoothing * inverse_scale * inverse_scale
    offset_high = float(np.float32(np.asarray(offset, BF16)))
    ones = jnp.where((row == 0) | (row == 2) | (row == 3), 1.0, 0.0)
    offsets = jnp.where(row == 1, 1.0, jnp.where(row == 2, offset_high, jnp.where(row == 3, offset - offset_high, 0.0)))
    source = [jnp.where(row < 6, parts, 1.0), jnp.where(row < 6, parts, squares), jnp.where(row == 1, s2, ones), zero]
    target = [
        jnp.where(row < 6, -2.0 * parts, squares),
        jnp.where(row < 6, -2.0 * swapped, 1.0),
        jnp.where(row == 0, s2, offsets),
        zero,
    ]
    return jnp.concatenate(source, 0).astype(BF16).T, jnp.concatenate(target, 0).astype(BF16)


def inverse_root(distance):
    return lax.rsqrt(distance).astype(BF16)


def pack_kernel(place, points_hbm, values_hbm, first, second, points, values, sems):
    copies = [
        pltpu.make_async_copy(points_hbm, points, sems.at[0]),
        pltpu.make_async_copy(values_hbm, values, sems.at[1]),
    ]
    for copy in copies:
        copy.start()
    for copy in copies:
        copy.wait()
    odd = lax.bitwise_and(place[0], 1)
    width = 4 * LEAF
    for out, side in ((first, 1 - odd), (second, odd)):
        for j in range(EDGE // 4):
            some = aligned(side * (EDGE // 4) + j, width)
            rows = jnp.concatenate([values[:, some], split_points(points[:, some])], 0)
            out[:, j * width : (j + 1) * width] = rows.astype(BF16)


def top_bit(x):
    return jnp.maximum(31 - lax.clz(x), 0)


def node_of(owner, level):
    return 2 * OWN - 2 * (OWN >> level) + lax.shift_right_logical(owner, level)


def path_copies(table, rows, owner, sems, first):
    copies = []
    for level in range(5):
        start = pl.multiple_of(lax.shift_right_logical(node_of(owner, level), 3) * 8, 8)
        copies.append(pltpu.make_async_copy(table.at[pl.ds(start, 8)], rows.at[level], sems.at[first + level]))
    copies.append(pltpu.make_async_copy(table.at[pl.ds(248, 6)], rows.at[5, pl.ds(0, 6)], sems.at[first + 5]))
    return copies


def path_matrix(rows, owner, level, matrices, slot):
    node = node_of(owner, level)
    fetch(rows.at[min(level, 5)], lax.bitwise_and(node, 7), matrices, slot)


def moment_kernel(
    place, send_leaf, send_count, values_hbm, basis_hbm, transfer_hbm, top_transfer_hbm,
    message, values, basis, transfer, rows, moments, chain, matrices, sems,
):
    owner = place[0]
    chunks = 8
    chunk = OWN // chunks
    copies = []
    for i in range(chunks):
        some = pl.ds(i * chunk * LEAF, chunk * LEAF)
        copies.append(pltpu.make_async_copy(values_hbm.at[:, some], values.at[:, some], sems.at[3 * i]))
        some = pl.ds(i * chunk, chunk)
        copies.append(pltpu.make_async_copy(basis_hbm.at[some], basis.at[some], sems.at[3 * i + 1]))
        some = pl.ds(i * chunk * R, chunk * R)
        copies.append(pltpu.make_async_copy(transfer_hbm.at[:, some], transfer.at[:, some], sems.at[3 * i + 2]))
    paths = path_copies(top_transfer_hbm, rows, owner, sems, 3 * chunks)
    for copy in copies + paths:
        copy.start()

    def some_leaves(g, total):
        picked = []
        for j in range(16):
            leaf = g * 16 + j
            v = values[:, aligned(leaf, LEAF)].astype(BF16)
            picked.append(round16(dot(v, basis[leaf], NT)))
        for j in range(16):
            moments[g * 16 + j] = jnp.concatenate([picked[j], picked[j]], 1)
        for j in range(0, 16, 4):
            four = jnp.concatenate(picked[j : j + 4], 0).astype(BF16)
            total = total + dot(four, transfer[:, aligned(g * 4 + j // 4, 4 * R)])
        return total

    total = jnp.zeros((4 * N, 4 * R), F32)
    for i in range(chunks):
        for copy in copies[3 * i : 3 * i + 3]:
            copy.wait()
        total = lax.fori_loop(i * chunk // 16, (i + 1) * chunk // 16, some_leaves, total)
    current = total[0:N, 0:R]
    for j in range(1, 4):
        current = current + total[j * N : (j + 1) * N, j * R : (j + 1) * R]
    current = current * (1.0 / math.sqrt(OWN))

    for copy in paths:
        copy.wait()
    for level in range(6):
        path_matrix(rows, owner, level, matrices, level)
    for level in range(7):
        high = round16(current)
        chain[level] = jnp.concatenate([high, current - high], 1)
        if level < 6:
            current = exact_dot(current, matrices[level])

    is_left = lax.broadcasted_iota(jnp.int32, (N, 2 * R), 1) < R

    def one_receiver(p, carry):
        parts = []
        count = send_count[0, p]
        for pair in range(SLOTS // 2):
            left = moments[send_leaf[2 * pair, 0, p]]
            right = moments[send_leaf[2 * pair + 1, 0, p]]
            left = jnp.where(2 * pair < count, left, 0.0)
            right = jnp.where(2 * pair + 1 < count, right, 0.0)
            parts.append(jnp.where(is_left, left, right))
        parts.append(chain[top_bit(owner ^ p)])
        message[aligned(p, 4 * N), :] = jnp.concatenate(parts, 0).astype(BF16)
        return carry

    lax.fori_loop(0, OWN, one_receiver, 0, unroll=8)


def near_kernel(
    place, near_list, first, second, points_hbm, values_hbm, out, points, values, sources, targets, seen_values, sems,
):
    copies = [
        pltpu.make_async_copy(points_hbm, points, sems.at[0]),
        pltpu.make_async_copy(values_hbm, values, sems.at[1]),
    ]
    for copy in copies:
        copy.start()
    odd = lax.bitwise_and(place[0], 1)

    def rim(ref, start):
        def one(i, carry):
            block = ref[:, aligned(i, LEAF)].astype(F32)
            sources[start + i] = features(block[N:, :])[0]
            seen_values[start + i] = block[:N, :]
            return carry

        lax.fori_loop(0, EDGE, one, 0, unroll=16)

    def own(i, carry):
        parts = split_points(points[:, aligned(i, LEAF)])
        sources[EDGE + i], targets[i] = features(parts)
        seen_values[EDGE + i] = values[:, aligned(i, LEAF)]
        return carry

    rim(first, (1 - odd) * (EDGE + OWN))
    rim(second, odd * (EDGE + OWN))
    for copy in copies:
        copy.wait()
    lax.fori_loop(0, OWN, own, 0, unroll=16)

    def sixteen_leaves(g, carry):
        pairs = []
        for j in range(16):
            leaf = g * 16 + j
            seen = [EDGE + leaf] + [near_list[k, leaf] for k in range(NEAR)]
            pairs.extend((leaf, (j, k), e) for k, e in enumerate(seen))
        groups = [pairs[i : i + 8] for i in range(0, len(pairs), 8)]
        kernels = {}
        total = None
        for ahead, now in zip(groups + [[]], [[]] + groups):
            for i in range(0, 8, 4):
                for leaf, pair, e in ahead[i : i + 4]:
                    kernels[pair] = inverse_root(dot(sources[e], targets[leaf]))
                for leaf, pair, e in now[i : i + 4]:
                    part = dot(seen_values[e].astype(BF16), kernels.pop(pair))
                    total = part if pair[1] == 0 else total + part
                    if pair[1] == NEAR:
                        out[:, aligned(leaf, LEAF)] = total
        return carry

    lax.fori_loop(0, OWN // 16, sixteen_leaves, 0)


def fetch(table, row, matrices, slot):
    flat = table[pl.ds(row, 1), :]
    for j in range(R // 2):
        pair = flat[:, j * 2 * R : (j + 1) * 2 * R]
        matrices[slot, 2 * j : 2 * j + 1, 0:R] = pair[:, 0:R]
        matrices[slot, 2 * j + 1 : 2 * j + 2, 0:R] = pair[:, R : 2 * R]


def far_kernel(
    place, far_target, incoming, near_hbm,
    coupling_hbm, transfer_hbm, basis_hbm, top_transfer_hbm, top_coupling_hbm,
    out_hbm,
    near, out, coupling, transfer, basis, transfer_rows, coupling_rows, far_local, matrices, siblings, sems,
):
    owner = place[0]
    chunks = 8
    chunk = OWN // chunks
    copies = []
    for i in range(chunks):
        some = pl.ds(i * chunk, chunk)
        copies.append(pltpu.make_async_copy(coupling_hbm.at[some], coupling.at[some], sems.at[i]))
    paths = path_copies(top_transfer_hbm, transfer_rows, owner, sems, chunks)
    paths = paths + path_copies(top_coupling_hbm, coupling_rows, owner, sems, chunks + 6)
    first = chunks + 12
    rest = [
        pltpu.make_async_copy(source, target, sems.at[first + i])
        for i, (source, target) in enumerate([(transfer_hbm, transfer), (basis_hbm, basis), (near_hbm, near)])
    ]
    for copy in copies + paths + rest:
        copy.start()

    far_local[...] = jnp.zeros_like(far_local)
    siblings[...] = jnp.zeros_like(siblings)
    is_left = lax.broadcasted_iota(jnp.int32, (N, 2 * R), 1) < R

    for i in range(chunks):
        copies[i].wait()

        def two_senders(g, carry):
            arrived = incoming[aligned(g, 64), :].astype(F32)
            results = []
            for j in range(2):
                p = g * 2 + j
                for pair in range(SLOTS // 2):
                    tile = arrived[(j * 4 + pair) * N : (j * 4 + pair + 1) * N, :]
                    left = jnp.where(is_left, tile, 0.0)
                    right = jnp.where(is_left, 0.0, tile)
                    both = jnp.concatenate([left, right], 0).astype(BF16)
                    matrix = coupling[p, :, pair * 2 * R : (pair + 1) * 2 * R]
                    results.append(dot(both, matrix, NT))
            for j in range(2):
                p = g * 2 + j
                level = jnp.where(p == owner, 7, top_bit(owner ^ p))
                siblings[level] = siblings[level] + arrived[(j * 4 + 3) * N : (j * 4 + 4) * N, :]
                for slot in range(SLOTS):
                    leaf = far_target[slot, 0, p]
                    part = results[j * 3 + slot // 2][(slot % 2) * N : (slot % 2 + 1) * N, :]
                    far_local[leaf] = far_local[leaf] + part
            return carry

        lax.fori_loop(i * chunk // 2, (i + 1) * chunk // 2, two_senders, 0, unroll=8)

    for copy in paths:
        copy.wait()
    for level in range(7):
        path_matrix(coupling_rows, owner, level, matrices, level)
        if level < 6:
            path_matrix(transfer_rows, owner, level, matrices, 7 + level)
    coupled = []
    for level in range(7):
        both = siblings[level]
        coupled.append(exact_dot(both[:, :R] + both[:, R:], matrices[level], NT))
    field = coupled[6]
    for level in reversed(range(6)):
        field = coupled[level] + exact_dot(field, matrices[7 + level], NT)
    field = round16(field)

    wide = jnp.concatenate([jnp.concatenate([field] * 4, 1)] * 4, 0)
    row_leaf = lax.broadcasted_iota(jnp.int32, (4 * N, 4 * R), 0) // N
    column_leaf = lax.broadcasted_iota(jnp.int32, (4 * N, 4 * R), 1) // R
    fields = jnp.where(row_leaf == column_leaf, wide, 0.0).astype(BF16)
    for copy in rest:
        copy.wait()

    def some_leaves(g, carry):
        locals_ = []
        for i in range(4):
            locals_.append(dot(fields, transfer[:, aligned(g * 4 + i, 4 * R)], NT))
        for j in range(16):
            leaf = g * 16 + j
            total = (locals_[j // 4][(j % 4) * N : (j % 4 + 1) * N, :] + far_local[leaf]).astype(BF16)
            out[:, aligned(leaf, LEAF)] = near[:, aligned(leaf, LEAF)] + dot(total, basis[leaf])
        return carry

    results = []
    for i in range(chunks):
        lax.fori_loop(i * chunk // 16, (i + 1) * chunk // 16, some_leaves, 0)
        some = pl.ds(i * chunk * LEAF, chunk * LEAF)
        results.append(pltpu.make_async_copy(out.at[:, some], out_hbm.at[:, some], sems.at[first + 3 + i]))
        results[-1].start()
    for copy in results:
        copy.wait()


def swapped(block, axis, start):
    lower = range(start, lax.axis_size(axis) - 1, 2)
    return lax.ppermute(block, axis, [(i, i + 1) for i in lower] + [(i + 1, i) for i in lower])


def shards(
    positions, right_sides, leaf_basis, leaf_transfer, far_coupling, top_transfer, top_coupling,
    near_list, send_leaf, send_count, far_target,
):
    both = ("group", "dev")
    points = OWN * LEAF
    rim = EDGE * LEAF
    place = (lax.axis_index("group") * lax.axis_size("dev") + lax.axis_index("dev")).astype(jnp.int32).reshape(1)

    first, second = pl.pallas_call(
        pack_kernel,
        out_shape=(jax.ShapeDtypeStruct((2 * N, rim), BF16),) * 2,
        in_specs=[SMEM, HBM, HBM],
        out_specs=(VMEM, VMEM),
        scratch_shapes=[pltpu.VMEM((3, points), F32), pltpu.VMEM((N, points), F32), pltpu.SemaphoreType.DMA((2,))],
        compiler_params=params(63),
        cost_estimate=pl.CostEstimate(flops=10**7, bytes_accessed=3 << 20, transcendentals=0),
        name="pack",
    )(place, positions, right_sides)
    first = swapped(first, both, 0)
    second = swapped(second, both, 1)

    message = pl.pallas_call(
        moment_kernel,
        out_shape=jax.ShapeDtypeStruct((OWN * 4 * N, 2 * R), BF16),
        in_specs=[SMEM, SMEM, SMEM, HBM, HBM, HBM, HBM],
        out_specs=VMEM,
        scratch_shapes=[
            pltpu.VMEM((N, points), F32),
            pltpu.VMEM((OWN, R, LEAF), BF16),
            pltpu.VMEM((R, OWN * R), BF16),
            pltpu.VMEM((6, 8, R * R), F32),
            pltpu.VMEM((OWN, N, 2 * R), F32),
            pltpu.VMEM((7, N, 2 * R), F32),
            pltpu.VMEM((6, R, R), F32),
            pltpu.SemaphoreType.DMA((30,)),
        ],
        compiler_params=params(63),
        cost_estimate=pl.CostEstimate(flops=10**9, bytes_accessed=12 << 20, transcendentals=0),
        name="moments",
    )(place, send_leaf.transpose(2, 0, 1), send_count, right_sides, leaf_basis, leaf_transfer, top_transfer)
    incoming = lax.all_to_all(message, both, split_axis=0, concat_axis=0, tiled=True)

    near = pl.pallas_call(
        near_kernel,
        out_shape=jax.ShapeDtypeStruct((N, points), F32),
        in_specs=[SMEM, SMEM, VMEM, VMEM, HBM, HBM],
        out_specs=VMEM,
        scratch_shapes=[
            pltpu.VMEM((3, points), F32),
            pltpu.VMEM((N, points), F32),
            pltpu.VMEM((SEEN, LEAF, FEAT), BF16),
            pltpu.VMEM((OWN, FEAT, LEAF), BF16),
            pltpu.VMEM((SEEN, N, LEAF), F32),
            pltpu.SemaphoreType.DMA((2,)),
        ],
        compiler_params=params(63),
        cost_estimate=pl.CostEstimate(flops=60 * 10**9, bytes_accessed=6 << 20, transcendentals=0),
        name="near",
    )(place, near_list.T, first, second, positions, right_sides)

    return pl.pallas_call(
        far_kernel,
        out_shape=jax.ShapeDtypeStruct((N, points), F32),
        in_specs=[SMEM, SMEM, VMEM] + [HBM] * 6,
        out_specs=HBM,
        scratch_shapes=[
            pltpu.VMEM((N, points), F32),
            pltpu.VMEM((N, points), F32),
            pltpu.VMEM((OWN, R, SLOTS * R), BF16),
            pltpu.VMEM((R, OWN * R), BF16),
            pltpu.VMEM((OWN, R, LEAF), BF16),
            pltpu.VMEM((6, 8, R * R), F32),
            pltpu.VMEM((6, 8, R * R), F32),
            pltpu.VMEM((OWN, N, R), F32),
            pltpu.VMEM((13, R, R), F32),
            pltpu.VMEM((8, N, 2 * R), F32),
            pltpu.SemaphoreType.DMA((31,)),
        ],
        compiler_params=params(63),
        cost_estimate=pl.CostEstimate(flops=2 * 10**9, bytes_accessed=22 << 20, transcendentals=0),
        name="far_field",
    )(place, far_target.transpose(2, 0, 1), incoming, near, far_coupling[0], leaf_transfer, leaf_basis, top_transfer, top_coupling)


def solution(mesh):
    both = ("group", "dev")
    placed = (
        P(None, both), P(None, both), P(both, None, None), P(None, both), P(both, None, None, None),
        P(), P(), P(both, None), P(both, None, None), P(both, None), P(both, None, None),
    )
    return jax.shard_map(shards, mesh=mesh, in_specs=placed, out_specs=P(None, both), check_vma=False)
```

```python
import functools
import math

import jax
import jax.numpy as jnp
import numpy as np
from jax import lax
from jax.experimental import pallas as pl
from jax.experimental.pallas import tpu as pltpu
from jax.sharding import PartitionSpec as P

LEAF = 256
R = 64
N = 8
EDGE = 64
OWN = 128
SEEN = 256
SLOTS = 6
NEAR = 6
FEAT = 32
F32 = jnp.float32
BF16 = jnp.bfloat16

kernel_scale = 0.25 / (4.0 * math.pi)
smoothing = 0.0025
inverse_scale = 1.0 / kernel_scale

NN = (((1,), (0,)), ((), ()))
NT = (((1,), (1,)), ((), ()))
VMEM = pl.BlockSpec(memory_space=pltpu.VMEM)
SMEM = pl.BlockSpec(memory_space=pltpu.SMEM)
HBM = pl.BlockSpec(memory_space=pltpu.HBM)


def dot(a, b, dims=NN):
    return lax.dot_general(a, b, dims, preferred_element_type=F32)


def exact_dot(a, b, dims=NN):
    return lax.dot_general(a, b, dims, precision=lax.Precision.HIGHEST, preferred_element_type=F32)


def aligned(index, size):
    return pl.ds(pl.multiple_of(index * size, size), size)


def params(megabytes):
    return pltpu.CompilerParams(vmem_limit_bytes=megabytes << 20)


def round16(x):
    return x.astype(BF16).astype(F32)


def split_points(points):
    width = points.shape[1]
    row = lax.broadcasted_iota(jnp.int32, (N, width), 0)
    padded = jnp.concatenate([points, jnp.ones((5, width), F32)], 0)
    x = jnp.where(row < 3, (padded - 1.0) * inverse_scale, 0.0)
    high = round16(x)
    return high + pltpu.roll(round16(x - high), 3, 0)


def features(parts):
    row = lax.broadcasted_iota(jnp.int32, parts.shape, 0)
    swapped = jnp.where(row < 3, pltpu.roll(parts, 5, 0), pltpu.roll(parts, 3, 0))
    x = jnp.where(row < 3, parts + swapped, 0.0)
    square = x * x
    for shift in (4, 2, 1):
        square = square + pltpu.roll(square, shift, 0)
    s0 = round16(square)
    rest = square - s0
    s1 = round16(rest)
    s2 = rest - s1
    squares = jnp.where(row == 6, s0, s1)
    zero = jnp.zeros_like(parts)
    offset = smoothing * inverse_scale * inverse_scale
    offset_high = float(np.float32(np.asarray(offset, BF16)))
    ones = jnp.where((row == 0) | (row == 2) | (row == 3), 1.0, 0.0)
    offsets = jnp.where(row == 1, 1.0, jnp.where(row == 2, offset_high, jnp.where(row == 3, offset - offset_high, 0.0)))
    source = [jnp.where(row < 6, parts, 1.0), jnp.where(row < 6, parts, squares), jnp.where(row == 1, s2, ones), zero]
    target = [
        jnp.where(row < 6, -2.0 * parts, squares),
        jnp.where(row < 6, -2.0 * swapped, 1.0),
        jnp.where(row == 0, s2, offsets),
        zero,
    ]
    return jnp.concatenate(source, 0).astype(BF16).T, jnp.concatenate(target, 0).astype(BF16)


def inverse_root(distance):
    return lax.rsqrt(distance).astype(BF16)


def pack_kernel(place, points_hbm, values_hbm, first, second, points, values, sems):
    copies = [
        pltpu.make_async_copy(points_hbm, points, sems.at[0]),
        pltpu.make_async_copy(values_hbm, values, sems.at[1]),
    ]
    for copy in copies:
        copy.start()
    for copy in copies:
        copy.wait()
    odd = lax.bitwise_and(place[0], 1)
    width = 4 * LEAF
    for out, side in ((first, 1 - odd), (second, odd)):
        for j in range(EDGE // 4):
            some = aligned(side * (EDGE // 4) + j, width)
            rows = jnp.concatenate([values[:, some], split_points(points[:, some])], 0)
            out[:, j * width : (j + 1) * width] = rows.astype(BF16)


def top_bit(x):
    return jnp.maximum(31 - lax.clz(x), 0)


def node_of(owner, level):
    return 2 * OWN - 2 * (OWN >> level) + lax.shift_right_logical(owner, level)


def path_copies(table, rows, owner, sems, first):
    copies = []
    for level in range(5):
        start = pl.multiple_of(lax.shift_right_logical(node_of(owner, level), 3) * 8, 8)
        copies.append(pltpu.make_async_copy(table.at[pl.ds(start, 8)], rows.at[level], sems.at[first + level]))
    copies.append(pltpu.make_async_copy(table.at[pl.ds(248, 6)], rows.at[5, pl.ds(0, 6)], sems.at[first + 5]))
    return copies


def path_matrix(rows, owner, level, matrices, slot):
    node = node_of(owner, level)
    fetch(rows.at[min(level, 5)], lax.bitwise_and(node, 7), matrices, slot)


def moment_kernel(
    place, send_leaf, send_count, values_hbm, basis_hbm, transfer_hbm, top_transfer_hbm,
    message, values, basis, transfer, rows, moments, chain, matrices, sems,
):
    owner = place[0]
    chunks = 8
    chunk = OWN // chunks
    copies = []
    for i in range(chunks):
        some = pl.ds(i * chunk * LEAF, chunk * LEAF)
        copies.append(pltpu.make_async_copy(values_hbm.at[:, some], values.at[:, some], sems.at[3 * i]))
        some = pl.ds(i * chunk, chunk)
        copies.append(pltpu.make_async_copy(basis_hbm.at[some], basis.at[some], sems.at[3 * i + 1]))
        some = pl.ds(i * chunk * R, chunk * R)
        copies.append(pltpu.make_async_copy(transfer_hbm.at[:, some], transfer.at[:, some], sems.at[3 * i + 2]))
    paths = path_copies(top_transfer_hbm, rows, owner, sems, 3 * chunks)
    for copy in copies + paths:
        copy.start()

    def some_leaves(g, total):
        picked = []
        for j in range(16):
            leaf = g * 16 + j
            v = values[:, aligned(leaf, LEAF)].astype(BF16)
            picked.append(round16(dot(v, basis[leaf], NT)))
        for j in range(16):
            moments[g * 16 + j] = jnp.concatenate([picked[j], picked[j]], 1)
        for j in range(0, 16, 4):
            four = jnp.concatenate(picked[j : j + 4], 0).astype(BF16)
            total = total + dot(four, transfer[:, aligned(g * 4 + j // 4, 4 * R)])
        return total

    total = jnp.zeros((4 * N, 4 * R), F32)
    for i in range(chunks):
        for copy in copies[3 * i : 3 * i + 3]:
            copy.wait()
        total = lax.fori_loop(i * chunk // 16, (i + 1) * chunk // 16, some_leaves, total)
    current = total[0:N, 0:R]
    for j in range(1, 4):
        current = current + total[j * N : (j + 1) * N, j * R : (j + 1) * R]
    current = current * (1.0 / math.sqrt(OWN))

    for copy in paths:
        copy.wait()
    for level in range(6):
        path_matrix(rows, owner, level, matrices, level)
    for level in range(7):
        high = round16(current)
        chain[level] = jnp.concatenate([high, current - high], 1)
        if level < 6:
            current = exact_dot(current, matrices[level])

    is_left = lax.broadcasted_iota(jnp.int32, (N, 2 * R), 1) < R

    def one_receiver(p, carry):
        parts = []
        count = send_count[0, p]
        for pair in range(SLOTS // 2):
            left = moments[send_leaf[2 * pair, 0, p]]
            right = moments[send_leaf[2 * pair + 1, 0, p]]
            left = jnp.where(2 * pair < count, left, 0.0)
            right = jnp.where(2 * pair + 1 < count, right, 0.0)
            parts.append(jnp.where(is_left, left, right))
        parts.append(chain[top_bit(owner ^ p)])
        message[aligned(p, 4 * N), :] = jnp.concatenate(parts, 0).astype(BF16)
        return carry

    lax.fori_loop(0, OWN, one_receiver, 0, unroll=8)


def near_kernel(
    place, near_list, first, second, points_hbm, values_hbm, out, points, values, sources, targets, seen_values, sems,
):
    copies = [
        pltpu.make_async_copy(points_hbm, points, sems.at[0]),
        pltpu.make_async_copy(values_hbm, values, sems.at[1]),
    ]
    for copy in copies:
        copy.start()
    odd = lax.bitwise_and(place[0], 1)

    def rim(ref, start):
        def one(i, carry):
            block = ref[:, aligned(i, LEAF)].astype(F32)
            sources[start + i] = features(block[N:, :])[0]
            seen_values[start + i] = block[:N, :]
            return carry

        lax.fori_loop(0, EDGE, one, 0, unroll=32)

    def own(i, carry):
        parts = split_points(points[:, aligned(i, LEAF)])
        sources[EDGE + i], targets[i] = features(parts)
        seen_values[EDGE + i] = values[:, aligned(i, LEAF)]
        return carry

    rim(first, (1 - odd) * (EDGE + OWN))
    rim(second, odd * (EDGE + OWN))
    for copy in copies:
        copy.wait()
    lax.fori_loop(0, OWN, own, 0, unroll=32)

    def many_leaves(g, carry):
        pairs = []
        for j in range(32):
            leaf = g * 32 + j
            seen = [EDGE + leaf] + [near_list[k, leaf] for k in range(NEAR)]
            pairs.extend((leaf, (j, k), e) for k, e in enumerate(seen))
        groups = [pairs[i : i + 8] for i in range(0, len(pairs), 8)]
        kernels = {}
        total = None
        for ahead, now in zip(groups + [[]], [[]] + groups):
            for i in range(0, 8, 4):
                for leaf, pair, e in ahead[i : i + 4]:
                    kernels[pair] = inverse_root(dot(sources[e], targets[leaf]))
                for leaf, pair, e in now[i : i + 4]:
                    part = dot(seen_values[e].astype(BF16), kernels.pop(pair))
                    total = part if pair[1] == 0 else total + part
                    if pair[1] == NEAR:
                        out[:, aligned(leaf, LEAF)] = total
        return carry

    lax.fori_loop(0, OWN // 32, many_leaves, 0)


def fetch(table, row, matrices, slot):
    flat = table[pl.ds(row, 1), :]
    for j in range(R // 2):
        pair = flat[:, j * 2 * R : (j + 1) * 2 * R]
        matrices[slot, 2 * j : 2 * j + 1, 0:R] = pair[:, 0:R]
        matrices[slot, 2 * j + 1 : 2 * j + 2, 0:R] = pair[:, R : 2 * R]


def far_kernel(
    place, far_target, incoming, near_hbm,
    coupling_hbm, transfer_hbm, basis_hbm, top_transfer_hbm, top_coupling_hbm,
    out_hbm,
    near, out, coupling, transfer, basis, transfer_rows, coupling_rows, far_local, matrices, siblings, sems,
):
    owner = place[0]
    chunks = 8
    chunk = OWN // chunks
    copies = []
    for i in range(chunks):
        some = pl.ds(i * chunk, chunk)
        copies.append(pltpu.make_async_copy(coupling_hbm.at[some], coupling.at[some], sems.at[i]))
    paths = path_copies(top_transfer_hbm, transfer_rows, owner, sems, chunks)
    paths = paths + path_copies(top_coupling_hbm, coupling_rows, owner, sems, chunks + 6)
    first = chunks + 12
    rest = [
        pltpu.make_async_copy(source, target, sems.at[first + i])
        for i, (source, target) in enumerate([(transfer_hbm, transfer), (basis_hbm, basis), (near_hbm, near)])
    ]
    for copy in copies + paths + rest:
        copy.start()

    far_local[...] = jnp.zeros_like(far_local)
    siblings[...] = jnp.zeros_like(siblings)
    is_left = lax.broadcasted_iota(jnp.int32, (N, 2 * R), 1) < R

    for i in range(chunks):
        copies[i].wait()

        def two_senders(g, carry):
            arrived = incoming[aligned(g, 64), :].astype(F32)
            results = []
            for j in range(2):
                p = g * 2 + j
                for pair in range(SLOTS // 2):
                    tile = arrived[(j * 4 + pair) * N : (j * 4 + pair + 1) * N, :]
                    left = jnp.where(is_left, tile, 0.0)
                    right = jnp.where(is_left, 0.0, tile)
                    both = jnp.concatenate([left, right], 0).astype(BF16)
                    matrix = coupling[p, :, pair * 2 * R : (pair + 1) * 2 * R]
                    results.append(dot(both, matrix, NT))
            for j in range(2):
                p = g * 2 + j
                level = jnp.where(p == owner, 7, top_bit(owner ^ p))
                siblings[level] = siblings[level] + arrived[(j * 4 + 3) * N : (j * 4 + 4) * N, :]
                for slot in range(SLOTS):
                    leaf = far_target[slot, 0, p]
                    part = results[j * 3 + slot // 2][(slot % 2) * N : (slot % 2 + 1) * N, :]
                    far_local[leaf] = far_local[leaf] + part
            return carry

        lax.fori_loop(i * chunk // 2, (i + 1) * chunk // 2, two_senders, 0, unroll=8)

    for copy in paths:
        copy.wait()
    for level in range(7):
        path_matrix(coupling_rows, owner, level, matrices, level)
        if level < 6:
            path_matrix(transfer_rows, owner, level, matrices, 7 + level)
    coupled = []
    for level in range(7):
        both = siblings[level]
        coupled.append(exact_dot(both[:, :R] + both[:, R:], matrices[level], NT))
    field = coupled[6]
    for level in reversed(range(6)):
        field = coupled[level] + exact_dot(field, matrices[7 + level], NT)
    field = round16(field)

    wide = jnp.concatenate([jnp.concatenate([field] * 4, 1)] * 4, 0)
    row_leaf = lax.broadcasted_iota(jnp.int32, (4 * N, 4 * R), 0) // N
    column_leaf = lax.broadcasted_iota(jnp.int32, (4 * N, 4 * R), 1) // R
    fields = jnp.where(row_leaf == column_leaf, wide, 0.0).astype(BF16)
    for copy in rest:
        copy.wait()

    def some_leaves(g, carry):
        locals_ = []
        for i in range(4):
            locals_.append(dot(fields, transfer[:, aligned(g * 4 + i, 4 * R)], NT))
        for j in range(16):
            leaf = g * 16 + j
            total = (locals_[j // 4][(j % 4) * N : (j % 4 + 1) * N, :] + far_local[leaf]).astype(BF16)
            out[:, aligned(leaf, LEAF)] = near[:, aligned(leaf, LEAF)] + dot(total, basis[leaf])
        return carry

    results = []
    for i in range(chunks):
        lax.fori_loop(i * chunk // 16, (i + 1) * chunk // 16, some_leaves, 0)
        some = pl.ds(i * chunk * LEAF, chunk * LEAF)
        results.append(pltpu.make_async_copy(out.at[:, some], out_hbm.at[:, some], sems.at[first + 3 + i]))
        results[-1].start()
    for copy in results:
        copy.wait()


def swapped(block, axis, start):
    lower = range(start, lax.axis_size(axis) - 1, 2)
    return lax.ppermute(block, axis, [(i, i + 1) for i in lower] + [(i + 1, i) for i in lower])


def shards(
    positions, right_sides, leaf_basis, leaf_transfer, far_coupling, top_transfer, top_coupling,
    near_list, send_leaf, send_count, far_target,
):
    both = ("group", "dev")
    points = OWN * LEAF
    rim = EDGE * LEAF
    place = (lax.axis_index("group") * lax.axis_size("dev") + lax.axis_index("dev")).astype(jnp.int32).reshape(1)

    first, second = pl.pallas_call(
        pack_kernel,
        out_shape=(jax.ShapeDtypeStruct((2 * N, rim), BF16),) * 2,
        in_specs=[SMEM, HBM, HBM],
        out_specs=(VMEM, VMEM),
        scratch_shapes=[pltpu.VMEM((3, points), F32), pltpu.VMEM((N, points), F32), pltpu.SemaphoreType.DMA((2,))],
        compiler_params=params(63),
        cost_estimate=pl.CostEstimate(flops=10**7, bytes_accessed=3 << 20, transcendentals=0),
        name="pack",
    )(place, positions, right_sides)
    first = swapped(first, both, 0)
    second = swapped(second, both, 1)

    message = pl.pallas_call(
        moment_kernel,
        out_shape=jax.ShapeDtypeStruct((OWN * 4 * N, 2 * R), BF16),
        in_specs=[SMEM, SMEM, SMEM, HBM, HBM, HBM, HBM],
        out_specs=VMEM,
        scratch_shapes=[
            pltpu.VMEM((N, points), F32),
            pltpu.VMEM((OWN, R, LEAF), BF16),
            pltpu.VMEM((R, OWN * R), BF16),
            pltpu.VMEM((6, 8, R * R), F32),
            pltpu.VMEM((OWN, N, 2 * R), F32),
            pltpu.VMEM((7, N, 2 * R), F32),
            pltpu.VMEM((6, R, R), F32),
            pltpu.SemaphoreType.DMA((30,)),
        ],
        compiler_params=params(63),
        cost_estimate=pl.CostEstimate(flops=10**9, bytes_accessed=12 << 20, transcendentals=0),
        name="moments",
    )(place, send_leaf.transpose(2, 0, 1), send_count, right_sides, leaf_basis, leaf_transfer, top_transfer)
    incoming = lax.all_to_all(message, both, split_axis=0, concat_axis=0, tiled=True)

    near = pl.pallas_call(
        near_kernel,
        out_shape=jax.ShapeDtypeStruct((N, points), F32),
        in_specs=[SMEM, SMEM, VMEM, VMEM, HBM, HBM],
        out_specs=VMEM,
        scratch_shapes=[
            pltpu.VMEM((3, points), F32),
            pltpu.VMEM((N, points), F32),
            pltpu.VMEM((SEEN, LEAF, FEAT), BF16),
            pltpu.VMEM((OWN, FEAT, LEAF), BF16),
            pltpu.VMEM((SEEN, N, LEAF), F32),
            pltpu.SemaphoreType.DMA((2,)),
        ],
        compiler_params=params(63),
        cost_estimate=pl.CostEstimate(flops=60 * 10**9, bytes_accessed=6 << 20, transcendentals=0),
        name="near",
    )(place, near_list.T, first, second, positions, right_sides)

    return pl.pallas_call(
        far_kernel,
        out_shape=jax.ShapeDtypeStruct((N, points), F32),
        in_specs=[SMEM, SMEM, VMEM] + [HBM] * 6,
        out_specs=HBM,
        scratch_shapes=[
            pltpu.VMEM((N, points), F32),
            pltpu.VMEM((N, points), F32),
            pltpu.VMEM((OWN, R, SLOTS * R), BF16),
            pltpu.VMEM((R, OWN * R), BF16),
            pltpu.VMEM((OWN, R, LEAF), BF16),
            pltpu.VMEM((6, 8, R * R), F32),
            pltpu.VMEM((6, 8, R * R), F32),
            pltpu.VMEM((OWN, N, R), F32),
            pltpu.VMEM((13, R, R), F32),
            pltpu.VMEM((8, N, 2 * R), F32),
            pltpu.SemaphoreType.DMA((31,)),
        ],
        compiler_params=params(63),
        cost_estimate=pl.CostEstimate(flops=2 * 10**9, bytes_accessed=22 << 20, transcendentals=0),
        name="far_field",
    )(place, far_target.transpose(2, 0, 1), incoming, near, far_coupling[0], leaf_transfer, leaf_basis, top_transfer, top_coupling)


def solution(mesh):
    both = ("group", "dev")
    placed = (
        P(None, both), P(None, both), P(both, None, None), P(None, both), P(both, None, None, None),
        P(), P(), P(both, None), P(both, None, None), P(both, None), P(both, None, None),
    )
    return jax.shard_map(shards, mesh=mesh, in_specs=placed, out_specs=P(None, both), check_vma=False)
```
